256 devices in a mesh: rec: 16 (over y_lo, z), lig: 8 (over y_hi, x), slab: 2 (over core).
Axes of the slice: x: 4, y: 4 (y_hi: 2, y_lo: 2; y = y_hi * 2 + y_lo), z: 8, core: 2. Of those that a mesh axis runs over, the one named last changes fastest.
Arguments:
- receptors: float32 [16, 4, 64, 4096], P('rec', None, 'slab'), may hold values from -6 to 6
- ligands: float32 [128, 4, 64, 4096], P(('rec', 'lig'), None, 'slab'), may hold values from -6 to 6
- plan: int32 [1], replicated, may hold values from 0 to 15
- rotations: int32 [2], replicated, may hold values from 0 to 7
Outputs:
- scores: float32 [1, 2, 128, 64, 4096], P(None, None, ('rec', 'lig'), 'slab')
The draws below stay inside these ranges and needn't reach their ends.
All inputs are finite; a program needn't handle non-finite values.
Results may differ from the reference program's by a relative error of at most 0.0003.
Values sent between devices are 32-bit elements; how exact they have to be, the bound alone decides.
No kernel may reach another device: no remote copies, remote signals or barrier semaphores. Data moves between devices by JAX's collectives and lax.ppermute only.
A program may use at most 192 MiB of HBM per device.

```python
import math
from functools import partial
import jax
import jax.numpy as jnp
from jax import lax

G = 64
C = 4
ROTSET = 8
STEPS = 1
ROTS = 2
RECEPTORS = 16
LIGANDS = 128
N_REC = 16


def steps_of(rng, extent, shards, low, high):
    level, own = 1.0, jax.random.fold_in(rng, 6)
    for dim, blocks in shards:
        steps = jnp.exp(jax.random.uniform(jax.random.fold_in(own, dim), (blocks,), jnp.float32, low / len(shards), high / len(shards)))
        level = level * jnp.repeat(steps, extent[dim] // blocks).reshape([-1 if axis == dim else 1 for axis in range(len(extent))])
    return level


def noise(own_key, extent, width, limit, split=(), held_as=jnp.bfloat16):
    array = width * jax.random.normal(own_key, extent, jnp.float32)
    if split:
        array = array * steps_of(own_key, extent, split, -0.22, 0.18)
    return jnp.clip(array, -limit, limit).astype(held_as)


def setup_inputs(seed: int = 0) -> dict:
    key_of = jax.random.split(jax.random.key(seed), 5)
    return {
        "receptors": noise(key_of[0], (RECEPTORS, C, G, G * G), 1.0, 6.0, ((0, 16), (2, 2)), jnp.float32),
        "ligands": noise(key_of[1], (LIGANDS, C, G, G * G), 1.0, 6.0, ((0, 128), (2, 2)), jnp.float32),
        "plan": jax.random.randint(key_of[2], (STEPS,), 0, N_REC).astype(jnp.int32),
        "rotations": jax.random.randint(key_of[3], (ROTS,), 0, ROTSET).astype(jnp.int32),
    }


def reverse(values, along_axis):
    return jnp.roll(jnp.flip(values, along_axis), 1, along_axis)

def rotate_cube(grid_cube, quarter, mirrored):
    for turn_index in range(quarter):
        grid_cube = reverse(jnp.swapaxes(grid_cube, 1, 3), 1)
    if mirrored:
        grid_cube = reverse(reverse(grid_cube, 1), 2)
    return grid_cube

def reference(receptors, ligands, plan, rotations):
    branches = [partial(rotate_cube, quarter=turn_count % 4, mirrored=turn_count >= 4) for turn_count in range(ROTSET)]
    chosen = receptors[plan].reshape(STEPS, C, G, G, G)
    receptor_spectra = jnp.conj(jnp.fft.fftn(chosen, axes=(2, 3, 4)))
    factor = 1.0 / math.sqrt(C * G ** 3)

    def one_ligand(ligand):
        grid_cube = ligand.reshape(C, G, G, G)
        rotated = jnp.stack([lax.switch(rotations[slot_index], branches, grid_cube) for slot_index in range(ROTS)])
        spectra = jnp.fft.fftn(rotated, axes=(2, 3, 4))
        product = lax.optimization_barrier(jnp.sum(receptor_spectra[:, None] * spectra[None], axis=2))
        result = jnp.real(jnp.fft.ifftn(product, axes=(2, 3, 4))) * factor
        return result.reshape(STEPS, ROTS, G, G * G).astype(jnp.float32)
    results = lax.map(one_ligand, ligands)
    return jnp.transpose(results, (1, 2, 0, 3, 4))
```

```python
import math

import jax
import jax.numpy as jnp
import ml_dtypes
import numpy as np
from jax import lax
from jax.experimental import pallas as pl
from jax.experimental.pallas import tpu as pltpu
from jax.sharding import PartitionSpec as P

F32 = jnp.float32
BF16 = jnp.bfloat16


def split_table(table):
    high = table.astype(ml_dtypes.bfloat16)
    low = (table - high.astype(np.float64)).astype(ml_dtypes.bfloat16)
    return high, low


ROTATIONS = [
    (False, 1, 1, 1),
    (True, -1, 1, 1),
    (False, -1, 1, -1),
    (True, 1, 1, -1),
    (False, -1, -1, 1),
    (True, 1, -1, 1),
    (False, 1, -1, -1),
    (True, -1, -1, -1),
]


def dft(n):
    phase = np.outer(np.arange(n), np.arange(n)) % n * (2 * math.pi / n)
    return np.cos(phase), np.sin(phase)


def lane_table(n, swap, sy, sz):
    cos, sin = dft(n)
    eye = np.eye(2)
    real = np.concatenate([np.kron(eye, cos), np.kron(eye, -sz * sin)], axis=1)
    imag = np.concatenate([np.kron(eye, sy * sz * sin), np.kron(eye, sy * cos)], axis=1)
    table = np.concatenate([real, imag], axis=0)
    if swap:
        rows = table.reshape(2, 2, n, 4 * n)
        table = rows.transpose(1, 0, 2, 3).reshape(4 * n, 4 * n)
    return table


def row_table(n, sx):
    cos, sin = dft(n)
    return np.concatenate(
        [np.concatenate([cos, sx * sin], axis=1), np.concatenate([-sx * sin, cos], axis=1)], axis=0
    )


def lane_stack(table):
    high, low = split_table(table)
    return np.concatenate([high, high, low], axis=0)


def row_stack(table):
    high, low = split_table(table)
    return np.concatenate([high, low, high], axis=1)


def split(value):
    high = value.astype(BF16)
    return high, (value - high.astype(F32)).astype(BF16)


def lane_dot(value, table):
    high, low = split(value)
    return jnp.dot(
        jnp.concatenate([high, low, high], axis=1), table, preferred_element_type=F32
    )


def row_dot(table, value):
    high, low = split(value)
    return jnp.dot(
        table, jnp.concatenate([high, high, low], axis=0), preferred_element_type=F32
    )


def times_phase(value, cos, sin):
    re, im = value
    if im is None:
        return re * cos, -(re * sin)
    if abs(cos - sin) < 1e-12:
        return (re + im) * cos, (im - re) * cos
    return re * cos + im * sin, im * cos - re * sin


def real_forward(values):
    size = len(values)
    if size == 2:
        return [(values[0] + values[1], None), (values[0] - values[1], None)]
    even, odd = real_forward(values[0::2]), real_forward(values[1::2])
    out = [None] * (size // 2 + 1)
    out[0] = (even[0][0] + odd[0][0], None)
    out[size // 2] = (even[0][0] - odd[0][0], None)
    for k in range(1, size // 4):
        angle = 2 * math.pi * k / size
        re, im = times_phase(odd[k], math.cos(angle), math.sin(angle))
        out[k] = (even[k][0] + re, even[k][1] + im)
        out[size // 2 - k] = (even[k][0] - re, im - even[k][1])
    out[size // 4] = (even[size // 4][0], -odd[size // 4][0])
    return out


def real_inverse(spectrum):
    size = 2 * (len(spectrum) - 1)
    if size == 2:
        first, second = spectrum[0][0], spectrum[1][0]
        return [first + second, first - second]
    half, quarter = size // 2, size // 4
    even, odd = [None] * (quarter + 1), [None] * (quarter + 1)
    even[0] = (spectrum[0][0] + spectrum[half][0], None)
    odd[0] = (spectrum[0][0] - spectrum[half][0], None)
    for k in range(1, quarter):
        (ar, ai), (br, bi) = spectrum[k], spectrum[half - k]
        even[k] = (ar + br, ai - bi)
        angle = 2 * math.pi * k / size
        cos, sin = math.cos(angle), math.sin(angle)
        dr, di = ar - br, ai + bi
        if abs(cos - sin) < 1e-12:
            odd[k] = ((dr - di) * cos, (di + dr) * cos)
        else:
            odd[k] = (dr * cos - di * sin, di * cos + dr * sin)
    re, im = spectrum[quarter]
    even[quarter] = (re + re, None)
    odd[quarter] = (-(im + im), None)
    evens, odds = real_inverse(even), real_inverse(odd)
    return [value for pair in zip(evens, odds) for value in pair]


def lane_consts(width):
    left = lax.broadcasted_iota(jnp.int32, (8, width), 1) < width // 2
    one, zero = jnp.ones((8, width), F32), jnp.zeros((8, width), F32)
    return left, one, zero


def y_forward(load, count):
    width = 128
    left, one, zero = lane_consts(width)
    sign = jnp.where(left, one, -one)
    spectrum = real_forward([load(b) for b in range(count)])
    units = []
    first = spectrum[0][0]
    middle = spectrum[count // 2][0]
    units.append((first * sign + pltpu.roll(first, width // 2, 1), middle * sign))
    for k in range(1, count // 2):
        angle = 2 * math.pi * k / (2 * count)
        cos = jnp.where(left, one, math.cos(angle) * one)
        sin = jnp.where(left, zero, math.sin(angle) * one)
        re, im = spectrum[k]
        turned_re = re * cos + im * sin
        turned_im = im * cos - re * sin
        units.append(
            (
                turned_re * sign + pltpu.roll(turned_re, width // 2, 1),
                turned_im + pltpu.roll(turned_im, width // 2, 1) * sign,
            )
        )
    return units


def y_inverse(units):
    width = 128
    count = 2 * len(units)
    left, one, zero = lane_consts(width)
    sign = jnp.where(left, one, -one)
    spectrum = [None] * (count // 2 + 1)
    first, middle = units[0]
    spectrum[0] = (first * sign + pltpu.roll(first, width // 2, 1), None)
    spectrum[count // 2] = (middle * (sign + sign), None)
    for k in range(1, count // 2):
        angle = 2 * math.pi * k / (2 * count)
        cos = jnp.where(left, one, math.cos(angle) * one)
        sin = jnp.where(left, zero, math.sin(angle) * one)
        re, im = units[k]
        sum_re = re * sign + pltpu.roll(re, width // 2, 1)
        sum_im = im - pltpu.roll(im, width // 2, 1) * sign
        spectrum[k] = (sum_re * cos - sum_im * sin, sum_im * cos + sum_re * sin)
    return real_inverse(spectrum)


def forward_y_kernel(place_ref, grid_ref, mine_ref, other_ref):
    rows, width = grid_ref.shape
    count = width // 128

    def run(low_ref, high_ref):
        def step(tile, carry):
            at = pl.ds(pl.multiple_of(tile * 8, 8), 8)
            units = y_forward(lambda b: grid_ref[at, b * 128 : (b + 1) * 128], count)
            half = len(units) // 2
            for k, (re, im) in enumerate(units):
                out = low_ref if k < half else high_ref
                out[2 * (k % half), at, :] = re
                out[2 * (k % half) + 1, at, :] = im
            return carry

        lax.fori_loop(0, rows // 8, step, 0)

    @pl.when(place_ref[0] == 0)
    def _():
        run(mine_ref, other_ref)

    @pl.when(place_ref[0] == 1)
    def _():
        run(other_ref, mine_ref)


def forward_y(place, grid, block, steps, first):
    width = grid.shape[1]
    pieces = width // 256
    out = jax.ShapeDtypeStruct((pieces, block * steps, 128), F32)
    spec = pl.BlockSpec((pieces, block, 128), lambda i, place: (0, i, 0))
    return pl.pallas_call(
        forward_y_kernel,
        grid_spec=pltpu.PrefetchScalarGridSpec(
            num_scalar_prefetch=1,
            grid=(steps,),
            in_specs=[pl.BlockSpec((block, width), lambda i, place: (first(place) + i, 0))],
            out_specs=[spec, spec],
        ),
        out_shape=[out, out],
    )(place, grid)


def unit_tiles(step, place, first_re, first_im):
    odd = (place == 1).astype(F32)
    left = lax.broadcasted_iota(jnp.int32, first_re.shape, 1) < first_re.shape[1] // 2
    mask = jnp.where(left, 1.0 - odd, 0.0)
    rolled = pltpu.roll(first_im, first_im.shape[1] // 2, 1)
    keep = jnp.where(step == 1, odd, 1.0)
    extra = step == 0
    re = jnp.where(extra, first_im * mask, first_re)
    im = jnp.where(extra, rolled * mask, first_im * keep)
    return re, im


def spectrum_kernel(place_ref, turn_ref, mine_ref, other_ref, lane_ref, row_ref, out_ref, work):
    step = pl.program_id(1)
    slot = pl.program_id(0)
    place = place_ref[0]
    length = 64
    channels = mine_ref.shape[1] // 32
    swapped = lax.rem(turn_ref[slot], 2) == 1

    def tiles(c):
        at = pl.ds(c * 32, 32)
        own_re, own_im = mine_ref[0, at, :], mine_ref[1, at, :]
        far_re, far_im = other_ref[0, at, :], other_ref[1, at, :]
        is_low = place == 0
        re = jnp.concatenate(
            [jnp.where(is_low, own_re, far_re), jnp.where(is_low, far_re, own_re)], axis=0
        )
        im = jnp.concatenate(
            [jnp.where(is_low, own_im, far_im), jnp.where(is_low, far_im, own_im)], axis=0
        )
        return unit_tiles(step, place, re, im)

    @pl.when(jnp.logical_not(swapped))
    def _():
        for c in range(channels):
            re, im = tiles(c)
            work[c * 64 : (c + 1) * 64, :128] = re
            work[c * 64 : (c + 1) * 64, 128:] = im

    @pl.when(swapped)
    def _():
        for c in range(channels):
            re, im = tiles(c)
            turned = jnp.concatenate([re, im], axis=0).T
            work[c * 64 : (c + 1) * 64, :128] = turned[:length]
            work[c * 64 : (c + 1) * 64, 128:] = turned[length:]

    along = lane_dot(work[...], lane_ref[0])
    for c in range(channels):
        part = along[c * 64 : (c + 1) * 64]
        both = jnp.concatenate([part[:, :128], part[:, 128:]], axis=0)
        out_ref[0, 0, c] = row_dot(row_ref[0], both)


def spectrum(place, turns, mine, other, lane_tables, row_tables):
    pieces, rows, _ = mine.shape
    steps = pieces // 2 + 1
    slots = turns.shape[0]
    channels = rows // 32
    unit = pl.BlockSpec((2, rows, 128), lambda i, u, place, turns: (jnp.maximum(u - 1, 0), 0, 0))
    return pl.pallas_call(
        spectrum_kernel,
        grid_spec=pltpu.PrefetchScalarGridSpec(
            num_scalar_prefetch=2,
            grid=(slots, steps),
            in_specs=[
                unit,
                unit,
                pl.BlockSpec((1, 768, 256), lambda i, u, place, turns: (turns[i], 0, 0)),
                pl.BlockSpec((1, 128, 384), lambda i, u, place, turns: (turns[i], 0, 0)),
            ],
            out_specs=pl.BlockSpec(
                (1, 1, channels, 128, 128), lambda i, u, place, turns: (i, u, 0, 0, 0)
            ),
            scratch_shapes=[pltpu.VMEM((rows * 2, 256), F32)],
        ),
        out_shape=jax.ShapeDtypeStruct((slots, steps, channels, 128, 128), F32),
    )(place, turns, mine, other, lane_tables, row_tables)


def product_kernel(
    place_ref, rec_ref, lig_ref, lane_ref, row_ref, back_lane_ref, back_row_ref,
    mine_ref, other_ref, extra, planes,
):
    step = pl.program_id(0)
    place = place_ref[0]
    channels = lig_ref.shape[2]
    slots = lig_ref.shape[0]
    per = rec_ref.shape[0] // channels
    grids = []
    for c in range(channels):
        parts = [
            [rec_ref[c * per + p, part, s] for s in range(2) for p in range(per)] for part in range(2)
        ]
        re, im = (jnp.concatenate(piece, axis=0) for piece in parts)
        re, im = unit_tiles(step, place, re, im)
        grids.append(jnp.concatenate([re, im], axis=1))
    along = lane_dot(jnp.concatenate(grids, axis=0), lane_ref[...])
    sums = [None] * slots
    for c in range(channels):
        part = along[c * 64 : (c + 1) * 64]
        both = jnp.concatenate([part[:, :128], part[:, 128:]], axis=0)
        rec = row_dot(row_ref[...], both)
        rec_re, rec_im = rec[:64], rec[64:]
        for i in range(slots):
            re, im = lig_ref[i, 0, c, :64], lig_ref[i, 0, c, 64:]
            term = (rec_re * re + rec_im * im, rec_re * im - rec_im * re)
            sums[i] = term if c == 0 else (sums[i][0] + term[0], sums[i][1] + term[1])
    both = jnp.concatenate([jnp.concatenate(s, axis=0) for s in sums], axis=1)
    rows = row_dot(back_row_ref[...], both)
    lanes = jnp.concatenate(
        [
            jnp.concatenate([rows[:64, i * 128 : (i + 1) * 128], rows[64:, i * 128 : (i + 1) * 128]], axis=1)
            for i in range(slots)
        ],
        axis=0,
    )
    back = lane_dot(lanes, back_lane_ref[...])
    re, im = back[:, :128], back[:, 128:]

    @pl.when(step == 0)
    def _():
        left = lax.broadcasted_iota(jnp.int32, re.shape, 1) < 64
        extra[...] = jnp.where(left, re, pltpu.roll(im, 64, 1))

    @pl.when(step > 0)
    def _():
        first = jnp.logical_and(step == 1, place == 0)
        planes[0] = re.reshape(slots, 64, 128)
        planes[1] = jnp.where(first, extra[...], im).reshape(slots, 64, 128)
        own = pl.ds(pl.multiple_of(place * 32, 32), 32)
        far = pl.ds(pl.multiple_of(32 - place * 32, 32), 32)
        for part in range(2):
            for i in range(slots):
                mine_ref[part, i] = planes[part, i, own, :]
                other_ref[part, i] = planes[part, i, far, :]


def product(place, rec, lig, tables):
    slots, steps, channels = lig.shape[:3]
    pieces = rec.shape[1]
    out = jax.ShapeDtypeStruct((pieces, slots, 32, 128), F32)
    unit = lambda u, place: (jnp.maximum(u - 1, 0), 0, 0, 0)
    whole = lambda t: pl.BlockSpec(t.shape, lambda u, place: (0, 0))
    return pl.pallas_call(
        product_kernel,
        grid_spec=pltpu.PrefetchScalarGridSpec(
            num_scalar_prefetch=1,
            grid=(steps,),
            in_specs=[
                pl.BlockSpec(
                    (rec.shape[0], 2, 2, rec.shape[3], 128),
                    lambda u, place: (0, jnp.maximum(u - 1, 0), 0, 0, 0),
                ),
                pl.BlockSpec((slots, 1, channels, 128, 128), lambda u, place: (0, u, 0, 0, 0)),
                *[whole(t) for t in tables],
            ],
            out_specs=[pl.BlockSpec((2, slots, 32, 128), unit)] * 2,
            scratch_shapes=[
                pltpu.VMEM((slots * 64, 128), F32),
                pltpu.VMEM((2, slots, 64, 128), F32),
            ],
        ),
        out_shape=[out, out],
    )(place, rec, lig, *tables)


def inverse_y_kernel(place_ref, mine_ref, other_ref, out_ref):
    pieces, slots, rows, _ = mine_ref.shape
    is_low = place_ref[0] == 0

    def step(tile, carry):
        slot = tile // (rows // 8)
        at = pl.ds(pl.multiple_of(tile % (rows // 8) * 8, 8), 8)
        low, high = [], []
        for k in range(pieces // 2):
            own = [mine_ref[2 * k + part, slot, at, :] for part in range(2)]
            far = [other_ref[2 * k + part, slot, at, :] for part in range(2)]
            low.append(tuple(jnp.where(is_low, a, b) for a, b in zip(own, far)))
            high.append(tuple(jnp.where(is_low, b, a) for a, b in zip(own, far)))
        for b, value in enumerate(y_inverse(low + high)):
            out_ref[slot, at, b * 128 : (b + 1) * 128] = value
        return carry

    lax.fori_loop(0, slots * (rows // 8), step, 0)


def inverse_y(place, mine, other):
    pieces, slots, rows, _ = mine.shape
    return pl.pallas_call(
        inverse_y_kernel,
        grid_spec=pltpu.PrefetchScalarGridSpec(
            num_scalar_prefetch=1,
            grid=(1,),
            in_specs=[pl.BlockSpec(mine.shape, lambda i, place: (0, 0, 0, 0))] * 2,
            out_specs=pl.BlockSpec((slots, rows, pieces * 256), lambda i, place: (0, 0, 0)),
        ),
        out_shape=jax.ShapeDtypeStruct((slots, rows, pieces * 256), F32),
    )(place, mine, other)


def per_device(receptors, ligands, plan, rotations):
    _, channels, half, flat = ligands.shape
    length = 2 * half
    core = lax.axis_index("slab")
    lig_index = lax.axis_index("lig")
    place = jnp.stack([core, lig_index]).astype(jnp.int32)
    swap = lambda value: lax.ppermute(value, "slab", [(0, 1), (1, 0)])
    lane_tables = jnp.asarray(
        np.stack([lane_stack(lane_table(length, swapped, sy, sz)) for swapped, _, sy, sz in ROTATIONS])
    )
    row_tables = jnp.asarray(np.stack([row_stack(row_table(length, sx)) for _, sx, _, _ in ROTATIONS]))
    factor = 1.0 / (math.sqrt(channels * length**3) * length**3)
    tables = [
        jnp.asarray(lane_stack(lane_table(length, False, 1, 1))),
        jnp.asarray(row_stack(row_table(length, 1))),
        jnp.asarray(lane_stack(lane_table(length, False, 1, -1) * factor)),
        jnp.asarray(row_stack(row_table(length, -1))),
    ]

    rec_rows = receptors.reshape(channels * half, flat)
    share = channels * half // lax.axis_size("lig")
    rec_mine, rec_other = forward_y(place, rec_rows, share, 1, lambda place: place[1])
    rec_far = swap(rec_other)
    is_low = core == 0
    rec_share = jnp.stack(
        [jnp.where(is_low, rec_mine, rec_far), jnp.where(is_low, rec_far, rec_mine)], axis=1
    )
    scattered = lax.all_to_all(rec_share, "rec", split_axis=0, concat_axis=0)
    piece = lax.dynamic_index_in_dim(scattered, plan[0], 0, True)
    gathered = lax.all_to_all(
        jnp.broadcast_to(piece, rec_share.shape), "rec", split_axis=0, concat_axis=0
    )
    spread = lax.all_to_all(
        jnp.broadcast_to(gathered[None], (lax.axis_size("lig"), *gathered.shape)),
        "lig",
        split_axis=0,
        concat_axis=0,
    )

    lig_rows = ligands.reshape(channels * half, flat)
    lig_mine, lig_other = forward_y(place, lig_rows, half, channels, lambda place: 0)
    lig_far = swap(lig_other)
    lig_spec = spectrum(place, rotations, lig_mine, lig_far, lane_tables, row_tables)

    out_mine, out_other = product(place, spread, lig_spec, tables)
    out_far = swap(out_other)
    scores = inverse_y(place, out_mine, out_far)
    return scores[None, :, None]


def solution(mesh):
    return jax.shard_map(
        per_device,
        mesh=mesh,
        in_specs=(P("rec", None, "slab", None), P(("rec", "lig"), None, "slab", None), P(), P()),
        out_specs=P(None, None, ("rec", "lig"), "slab", None),
        check_vma=False,
    )
```

```python
import math

import jax
import jax.numpy as jnp
import numpy as np
from jax import lax
from jax.experimental import pallas as pl
from jax.experimental.pallas import tpu as pltpu
from jax.sharding import Mesh, PartitionSpec as P

F32 = jnp.float32
BF16 = jnp.bfloat16
VMEM = pl.BlockSpec(memory_space=pltpu.VMEM)
SMEM = pl.BlockSpec(memory_space=pltpu.SMEM)
UNROLL = 4
COLORS = 4


ROTATIONS = [
    (False, 1, 1, 1),
    (True, -1, 1, 1),
    (False, -1, 1, -1),
    (True, 1, 1, -1),
    (False, -1, -1, 1),
    (True, 1, -1, 1),
    (False, 1, -1, -1),
    (True, -1, -1, -1),
]


def dft(n):
    phase = np.outer(np.arange(n), np.arange(n)) % n * (2 * math.pi / n)
    return np.cos(phase), np.sin(phase)


def base_tables(n):
    cos, sin = dft(n)
    eye = np.eye(2)
    plain = np.block([[np.kron(eye, cos), np.kron(eye, -sin)], [np.kron(eye, sin), np.kron(eye, cos)]])
    turned = plain.reshape(2, 2, n, 4 * n).transpose(1, 0, 2, 3).reshape(4 * n, 4 * n)
    rows = np.block([[cos, sin], [-sin, cos]])
    return np.stack([plain, turned]).astype(np.float32), rows.astype(np.float32)


SIGNS = np.array([[signs[1], signs[2], signs[3]] for signs in ROTATIONS], np.float32)


def split(value):
    high = value.astype(BF16)
    return high, (value - high.astype(F32)).astype(BF16)


def lane_stack(table):
    high, low = split(table)
    return jnp.concatenate([high, high, low], axis=0)


def row_stack(table):
    high, low = split(table)
    return jnp.concatenate([high, low, high], axis=1)


def lane_dot(value, table):
    high, low = split(value)
    return jnp.dot(jnp.concatenate([high, low, high], axis=1), table, preferred_element_type=F32)


def row_dot(table, value):
    high, low = split(value)
    return jnp.dot(table, jnp.concatenate([high, high, low], axis=0), preferred_element_type=F32)


def times_phase(value, cos, sin):
    re, im = value
    if im is None:
        return re * cos, -(re * sin)
    if abs(cos - sin) < 1e-12:
        return (re + im) * cos, (im - re) * cos
    return re * cos + im * sin, im * cos - re * sin


def real_forward(values):
    size = len(values)
    if size == 2:
        return [(values[0] + values[1], None), (values[0] - values[1], None)]
    even, odd = real_forward(values[0::2]), real_forward(values[1::2])
    out = [None] * (size // 2 + 1)
    out[0] = (even[0][0] + odd[0][0], None)
    out[size // 2] = (even[0][0] - odd[0][0], None)
    for k in range(1, size // 4):
        angle = 2 * math.pi * k / size
        re, im = times_phase(odd[k], math.cos(angle), math.sin(angle))
        out[k] = (even[k][0] + re, even[k][1] + im)
        out[size // 2 - k] = (even[k][0] - re, im - even[k][1])
    out[size // 4] = (even[size // 4][0], -odd[size // 4][0])
    return out


def real_inverse(spectrum):
    size = 2 * (len(spectrum) - 1)
    if size == 2:
        first, second = spectrum[0][0], spectrum[1][0]
        return [first + second, first - second]
    half, quarter = size // 2, size // 4
    even, odd = [None] * (quarter + 1), [None] * (quarter + 1)
    even[0] = (spectrum[0][0] + spectrum[half][0], None)
    odd[0] = (spectrum[0][0] - spectrum[half][0], None)
    for k in range(1, quarter):
        (ar, ai), (br, bi) = spectrum[k], spectrum[half - k]
        even[k] = (ar + br, ai - bi)
        angle = 2 * math.pi * k / size
        cos, sin = math.cos(angle), math.sin(angle)
        dr, di = ar - br, ai + bi
        if abs(cos - sin) < 1e-12:
            odd[k] = ((dr - di) * cos, (di + dr) * cos)
        else:
            odd[k] = (dr * cos - di * sin, di * cos + dr * sin)
    re, im = spectrum[quarter]
    even[quarter] = (re + re, None)
    odd[quarter] = (-(im + im), None)
    evens, odds = real_inverse(even), real_inverse(odd)
    return [value for pair in zip(evens, odds) for value in pair]


def lane_consts(width):
    left = lax.broadcasted_iota(jnp.int32, (8, width), 1) < width // 2
    one, zero = jnp.ones((8, width), F32), jnp.zeros((8, width), F32)
    return left, one, zero


def y_forward(load, count):
    width = 128
    left, one, zero = lane_consts(width)
    sign = jnp.where(left, one, -one)
    spectrum = real_forward([load(b) for b in range(count)])
    units = []
    first = spectrum[0][0]
    middle = spectrum[count // 2][0]
    units.append((first * sign + pltpu.roll(first, width // 2, 1), middle * sign))
    for k in range(1, count // 2):
        angle = 2 * math.pi * k / (2 * count)
        cos = jnp.where(left, one, math.cos(angle) * one)
        sin = jnp.where(left, zero, math.sin(angle) * one)
        re, im = spectrum[k]
        turned_re = re * cos + im * sin
        turned_im = im * cos - re * sin
        units.append(
            (
                turned_re * sign + pltpu.roll(turned_re, width // 2, 1),
                turned_im + pltpu.roll(turned_im, width // 2, 1) * sign,
            )
        )
    return units


def y_inverse(units):
    width = 128
    count = 2 * len(units)
    left, one, zero = lane_consts(width)
    sign = jnp.where(left, one, -one)
    spectrum = [None] * (count // 2 + 1)
    first, middle = units[0]
    spectrum[0] = (first * sign + pltpu.roll(first, width // 2, 1), None)
    spectrum[count // 2] = (middle * (sign + sign), None)
    for k in range(1, count // 2):
        angle = 2 * math.pi * k / (2 * count)
        cos = jnp.where(left, one, math.cos(angle) * one)
        sin = jnp.where(left, zero, math.sin(angle) * one)
        re, im = units[k]
        sum_re = re * sign + pltpu.roll(re, width // 2, 1)
        sum_im = im - pltpu.roll(im, width // 2, 1) * sign
        spectrum[k] = (sum_re * cos - sum_im * sin, sum_im * cos + sum_re * sin)
    return real_inverse(spectrum)


def forward_y_kernel(place_ref, grid_ref, mine_ref, other_ref):
    count = grid_ref.shape[1] // 128
    rows = mine_ref.shape[1]

    def run(low_ref, high_ref):
        def step(tile, carry):
            at = pl.ds(pl.multiple_of(tile * 8, 8), 8)
            units = y_forward(lambda b: grid_ref[at, b * 128 : (b + 1) * 128], count)
            half = len(units) // 2
            for k, (re, im) in enumerate(units):
                out = low_ref if k < half else high_ref
                out[2 * (k % half), at, :] = re
                out[2 * (k % half) + 1, at, :] = im
            return carry

        lax.fori_loop(0, rows // 8, step, 0, unroll=UNROLL)

    @pl.when(place_ref[0] == 0)
    def _():
        run(mine_ref, other_ref)

    @pl.when(place_ref[0] == 1)
    def _():
        run(other_ref, mine_ref)


def forward_y(place, grid):
    rows, width = grid.shape
    out = jax.ShapeDtypeStruct((width // 256, rows, 128), F32)
    return pl.pallas_call(
        forward_y_kernel,
        in_specs=[SMEM, VMEM],
        out_specs=[VMEM, VMEM],
        out_shape=[out, out],
        compiler_params=pltpu.CompilerParams(vmem_limit_bytes=40 * 1024 * 1024),
    )(place, grid)


def forward_rec_kernel(place_ref, grid_ref, mine_ref, other_ref, rows_ref, sems):
    share = mine_ref.shape[1]
    count = grid_ref.shape[1] // 128
    copies = []
    for turn in range(COLORS):
        start = lax.rem(place_ref[1] + turn, COLORS) * 2 * share + place_ref[2] * share
        rows = pl.ds(pl.multiple_of(start, share), share)
        copies.append(pltpu.make_async_copy(grid_ref.at[rows, :], rows_ref.at[turn], sems.at[turn]))
        copies[-1].start()
    for copy in copies:
        copy.wait()

    def run(low_ref, high_ref):
        for turn in range(COLORS):
            for tile in range(share // 8):
                at = pl.ds(tile * 8, 8)
                units = y_forward(lambda b: rows_ref[turn, at, b * 128 : (b + 1) * 128], count)
                half = len(units) // 2
                for piece in range(2 * half):
                    if (2 * (piece // 8) + piece) % COLORS == turn:
                        low_ref[piece, at, :] = units[piece // 2][piece % 2]
                        high_ref[piece, at, :] = units[half + piece // 2][piece % 2]

    @pl.when(place_ref[0] == 0)
    def _():
        run(mine_ref, other_ref)

    @pl.when(place_ref[0] == 1)
    def _():
        run(other_ref, mine_ref)


def forward_rec(place, grid):
    rows, width = grid.shape
    share = rows // (2 * COLORS)
    out = jax.ShapeDtypeStruct((width // 256, share, 128), F32)
    return pl.pallas_call(
        forward_rec_kernel,
        in_specs=[SMEM, pl.BlockSpec(memory_space=pl.ANY)],
        out_specs=[VMEM, VMEM],
        scratch_shapes=[
            pltpu.VMEM((COLORS, share, width), F32),
            pltpu.SemaphoreType.DMA((COLORS,)),
        ],
        out_shape=[out, out],
        compiler_params=pltpu.CompilerParams(vmem_limit_bytes=40 * 1024 * 1024),
    )(place, grid)


def unit_tiles(step, odd, first_re, first_im):
    left = lax.broadcasted_iota(jnp.int32, first_re.shape, 1) < first_re.shape[1] // 2
    mask = jnp.where(left, 1.0 - odd, 0.0)
    rolled = pltpu.roll(first_im, first_im.shape[1] // 2, 1)
    keep = jnp.where(step == 0, odd, 1.0)
    extra = step == STEPS - 1
    re = jnp.where(extra, first_im * mask, first_re)
    im = jnp.where(extra, rolled * mask, first_im * keep)
    return re, im


def signed(table, rows, cols, down, right, both):
    row = lax.broadcasted_iota(jnp.int32, table.shape, 0) // rows % 2 == 0
    col = lax.broadcasted_iota(jnp.int32, table.shape, 1) // cols % 2 == 0
    return table * jnp.where(row, jnp.where(col, 1.0, right), jnp.where(col, down, both))


STEPS = 9
BATCH = 9


def rows_of(lanes):
    grids = [lanes[at : at + 64] for at in range(0, lanes.shape[0], 64)]
    return jnp.concatenate(
        [jnp.concatenate([g[:, k * 128 : (k + 1) * 128] for g in grids], axis=1) for k in range(2)], axis=0
    )


def lanes_of(rows):
    return jnp.concatenate(
        [
            jnp.concatenate([rows[:64, at : at + 128], rows[64:, at : at + 128]], axis=1)
            for at in range(0, rows.shape[1], 128)
        ],
        axis=0,
    )


def spectrum_kernel(place_ref, turn_ref, signs_ref, mine_ref, other_ref, lane_ref, row_ref, out_ref, lane_work):
    place = place_ref[0]
    odd = place.astype(F32)
    channels = mine_ref.shape[1] // 32
    slots = out_ref.shape[0]
    is_low = place == 0

    def tiles(step, c):
        unit = lax.rem(step, STEPS - 1)
        at = pl.ds(c * 32, 32)
        parts = []
        for part in range(2):
            own, far = mine_ref[2 * unit + part, at, :], other_ref[2 * unit + part, at, :]
            parts.append(
                jnp.concatenate([jnp.where(is_low, own, far), jnp.where(is_low, far, own)], axis=0)
            )
        return unit_tiles(step, odd, *parts)

    for slot in range(slots):
        turn = turn_ref[slot]
        sx, sy, sz = (signs_ref[turn, k] for k in range(3))
        row_table = row_stack(signed(row_ref[...], 64, 64, sx, sx, 1.0))

        def run(swapped):
            table = signed(lane_ref[int(swapped)], 64 if swapped else 128, 128, sy * sz, sz, sy)
            lane_work[...] = lane_stack(table)

            def step(count, carry):
                grids = []
                for d in range(BATCH):
                    for c in range(channels):
                        re, im = tiles(count * BATCH + d, c)
                        if swapped:
                            turned = jnp.concatenate([re, im], axis=0).T
                            re, im = turned[:64], turned[64:]
                        grids.append(jnp.concatenate([re, im], axis=1))
                along = lane_dot(jnp.concatenate(grids, axis=0), lane_work[...])
                done = row_dot(row_table, rows_of(along))
                for d in range(BATCH):
                    for c in range(channels):
                        at = (d * channels + c) * 128
                        out_ref[slot, count * BATCH + d, c] = done[:, at : at + 128]
                return carry

            lax.fori_loop(0, STEPS // BATCH, step, 0)

        @pl.when(lax.rem(turn, 2) == 0)
        def _():
            run(False)

        @pl.when(lax.rem(turn, 2) == 1)
        def _():
            run(True)


def spectrum(place, turns, signs, mine, other, lane, row):
    pieces, rows, _ = mine.shape
    slots = turns.shape[0]
    channels = rows // 32
    return pl.pallas_call(
        spectrum_kernel,
        in_specs=[SMEM, SMEM, SMEM, VMEM, VMEM, VMEM, VMEM],
        out_specs=VMEM,
        scratch_shapes=[pltpu.VMEM((768, 256), BF16)],
        out_shape=jax.ShapeDtypeStruct((slots, STEPS, channels, 128, 128), F32),
        compiler_params=pltpu.CompilerParams(vmem_limit_bytes=40 * 1024 * 1024),
    )(place, turns, signs, mine, other, lane, row)


def product_kernel(
    factor, place_ref, own_ref, up_a, up_b, far_a, far_b, down_a, down_b, lig_ref, lane_ref, row_ref,
    mine_ref, other_ref, lane_work, back_work, planes,
):
    place = place_ref[0]
    odd = place.astype(F32)
    slots, steps, channels = lig_ref.shape[:3]
    lane_work[...] = lane_stack(lane_ref[0])
    back_work[...] = lane_stack(signed(lane_ref[0] * factor, 128, 128, -1.0, -1.0, 1.0))
    row_table = row_stack(row_ref[...])
    back_row = row_stack(signed(row_ref[...], 64, 64, -1.0, -1.0, 1.0))
    own = pl.ds(pl.multiple_of(place * 32, 32), 32)
    far = pl.ds(pl.multiple_of(32 - place * 32, 32), 32)
    rest = [(up_a, up_b), (far_a, far_b), (down_a, down_b)]

    def tile(turn, piece):
        if turn == 0:
            ref, at = own_ref, 2 * piece
        else:
            half = own_ref.shape[0] // 4
            ref, at = rest[turn - 1][piece // half], 2 * (piece % half)
        return jnp.concatenate([ref[at + p, s] for s in range(2) for p in range(2)], axis=0)

    grids = []
    for u in range(steps):
        unit = u % (steps - 1)
        for turn in range(channels):
            re, im = unit_tiles(u, odd, tile(turn, 2 * unit), tile(turn, 2 * unit + 1))
            grids.append(jnp.concatenate([re, im], axis=1))
    along = lane_dot(jnp.concatenate(grids, axis=0), lane_work[...])
    rec = row_dot(row_table, rows_of(along))
    sums = []
    for u in range(steps):
        for i in range(slots):
            for turn in range(channels):
                c = lax.rem(place_ref[3] + turn, channels)
                at = (u * channels + turn) * 128
                rec_re, rec_im = rec[:64, at : at + 128], rec[64:, at : at + 128]
                re, im = lig_ref[i, u, c, :64], lig_ref[i, u, c, 64:]
                term = (rec_re * re + rec_im * im, rec_re * im - rec_im * re)
                total = term if turn == 0 else (total[0] + term[0], total[1] + term[1])
            sums.append(jnp.concatenate(total, axis=0))
    rows = row_dot(back_row, jnp.concatenate(sums, axis=1))
    back = lane_dot(lanes_of(rows), back_work[...])
    parts = [back[u * slots * 64 : (u + 1) * slots * 64] for u in range(steps)]
    re, im = parts[-1][:, :128], parts[-1][:, 128:]
    left = lax.broadcasted_iota(jnp.int32, re.shape, 1) < 64
    extra = jnp.where(left, re, pltpu.roll(im, 64, 1))
    for u in range(steps - 1):
        re, im = parts[u][:, :128], parts[u][:, 128:]
        if u == 0:
            im = jnp.where(place == 0, extra, im)
        for part, value in enumerate((re, im)):
            planes[2 * u + part] = value.reshape(slots, 64, 128)
            for i in range(slots):
                mine_ref[2 * u + part, i] = planes[2 * u + part, i, own, :]
                other_ref[2 * u + part, i] = planes[2 * u + part, i, far, :]


def product(place, rec, lig, lane, row, factor):
    slots = lig.shape[0]
    pieces = 2 * (lig.shape[1] - 1)
    out = jax.ShapeDtypeStruct((pieces, slots, 32, 128), F32)
    return pl.pallas_call(
        lambda *refs: product_kernel(factor, *refs),
        in_specs=[SMEM] + [VMEM] * (len(rec) + 3),
        out_specs=[VMEM, VMEM],
        scratch_shapes=[
            pltpu.VMEM((768, 256), BF16),
            pltpu.VMEM((768, 256), BF16),
            pltpu.VMEM((pieces, slots, 64, 128), F32),
        ],
        out_shape=[out, out],
        compiler_params=pltpu.CompilerParams(vmem_limit_bytes=40 * 1024 * 1024),
    )(place, *rec, lig, lane, row)


def inverse_y_kernel(place_ref, mine_ref, other_ref, out_ref):
    pieces, slots, rows, _ = mine_ref.shape
    is_low = place_ref[0] == 0

    def step(tile, carry):
        slot = tile // (rows // 8)
        at = pl.ds(pl.multiple_of(tile % (rows // 8) * 8, 8), 8)
        low, high = [], []
        for k in range(pieces // 2):
            own = [mine_ref[2 * k + part, slot, at, :] for part in range(2)]
            far = [other_ref[2 * k + part, slot, at, :] for part in range(2)]
            low.append(tuple(jnp.where(is_low, a, b) for a, b in zip(own, far)))
            high.append(tuple(jnp.where(is_low, b, a) for a, b in zip(own, far)))
        for b, value in enumerate(y_inverse(low + high)):
            out_ref[slot, at, b * 128 : (b + 1) * 128] = value
        return carry

    lax.fori_loop(0, slots * (rows // 8), step, 0, unroll=UNROLL)


def inverse_y(place, mine, other):
    pieces, slots, rows, _ = mine.shape
    return pl.pallas_call(
        inverse_y_kernel,
        in_specs=[SMEM, VMEM, VMEM],
        out_specs=VMEM,
        out_shape=jax.ShapeDtypeStruct((slots, rows, pieces * 256), F32),
        compiler_params=pltpu.CompilerParams(vmem_limit_bytes=40 * 1024 * 1024),
    )(place, mine, other)


RING_X, RING_Y, RING_Z = 4, 4, 8


def color(x, y, z):
    return (x + 2 * y + z) % COLORS


def color_groups():
    return [
        [
            ((yl * RING_Z + z) * 2 * RING_X + yh * RING_X + (c - color(0, yl, z)) % RING_X) * 2 + core
            for yl in range(2)
            for z in range(RING_Z)
            for yh in range(2)
        ]
        for c in range(COLORS)
        for core in range(2)
    ]


def shift_x(step):
    return [(yh * RING_X + x, yh * RING_X + (x + step) % RING_X) for yh in range(2) for x in range(RING_X)]


def shift_y(step):
    place = lambda y, x: (y % 2) * 2 * RING_X + (y // 2) * RING_X + x
    return [(place(y, x), place((y + step) % RING_Y, x)) for y in range(RING_Y) for x in range(RING_X)]


def shift_z(step):
    return [(z, (z + step) % RING_Z) for z in range(RING_Z)]


def per_device(receptors, ligands, plan, rotations):
    _, channels, half, flat = ligands.shape
    length = 2 * half
    core = lax.axis_index("slab")
    y_hi, x = lax.axis_index("lig") // RING_X, lax.axis_index("lig") % RING_X
    tone = color(x, lax.axis_index("yl"), lax.axis_index("z"))
    place = jnp.stack([core, x, y_hi, tone]).astype(jnp.int32)
    swap = lambda value: lax.ppermute(value, "slab", [(0, 1), (1, 0)])
    lane, row = (jnp.asarray(table) for table in base_tables(length))
    signs = jnp.asarray(SIGNS)
    factor = 1.0 / (math.sqrt(channels * length**3) * length**3)

    rec_mine, rec_other = forward_rec(place, receptors.reshape(channels * half, flat))
    rec_far = swap(rec_other)
    is_low = core == 0
    rec_share = jnp.stack(
        [jnp.where(is_low, rec_mine, rec_far), jnp.where(is_low, rec_far, rec_mine)], axis=1
    )
    scattered = lax.all_to_all(rec_share, ("yl", "z"), split_axis=0, concat_axis=0)
    piece = lax.dynamic_index_in_dim(scattered, plan[0], 0, True)

    lig_mine, lig_other = forward_y(place, ligands.reshape(channels * half, flat))
    lig_far = swap(lig_other)
    piece, lig_mine, lig_far = lax.optimization_barrier((piece, lig_mine, lig_far))

    groups = color_groups()
    block = lax.all_to_all(
        jnp.broadcast_to(piece, (len(groups[0]), *piece.shape[1:])),
        ("yl", "z", "lig", "slab"),
        split_axis=0,
        concat_axis=0,
        axis_index_groups=groups,
    )
    block, lig_mine, lig_far = lax.optimization_barrier((block, lig_mine, lig_far))
    first, second = jnp.split(block, 2)
    rec = [
        block,
        lax.ppermute(first, "lig", shift_x(-1)),
        lax.ppermute(second, "z", shift_z(-1)),
        lax.ppermute(first, ("yl", "lig"), shift_y(1)),
        lax.ppermute(second, ("yl", "lig"), shift_y(-1)),
        lax.ppermute(first, "lig", shift_x(1)),
        lax.ppermute(second, "z", shift_z(1)),
    ]
    lig_spec = spectrum(place, rotations, signs, lig_mine, lig_far, lane, row)

    out_mine, out_other = product(place, rec, lig_spec, lane, row, factor)
    out_far = swap(out_other)
    scores = inverse_y(place, out_mine, out_far)
    return scores[None, :, None]


def solution(mesh):
    fine = Mesh(mesh.devices.reshape(2, RING_Z, 2 * RING_X, 2), ("yl", "z", "lig", "slab"))
    return jax.shard_map(
        per_device,
        mesh=fine,
        in_specs=(P(("yl", "z"), None, "slab", None), P(("yl", "z", "lig"), None, "slab", None), P(), P()),
        out_specs=P(None, None, ("yl", "z", "lig"), "slab", None),
        check_vma=False,
    )
```

```python
import math

import jax
import jax.numpy as jnp
import numpy as np
from jax import lax
from jax.experimental import pallas as pl
from jax.experimental.pallas import tpu as pltpu
from jax.sharding import Mesh, PartitionSpec as P

F32 = jnp.float32
BF16 = jnp.bfloat16
VMEM = pl.BlockSpec(memory_space=pltpu.VMEM)
SMEM = pl.BlockSpec(memory_space=pltpu.SMEM)
UNROLL = 4
COLORS = 4


ROTATIONS = [
    (False, 1, 1, 1),
    (True, -1, 1, 1),
    (False, -1, 1, -1),
    (True, 1, 1, -1),
    (False, -1, -1, 1),
    (True, 1, -1, 1),
    (False, 1, -1, -1),
    (True, -1, -1, -1),
]


def dft(n):
    phase = np.outer(np.arange(n), np.arange(n)) % n * (2 * math.pi / n)
    return np.cos(phase), np.sin(phase)


def base_tables(n):
    cos, sin = dft(n)
    eye = np.eye(2)
    plain = np.block([[np.kron(eye, cos), np.kron(eye, -sin)], [np.kron(eye, sin), np.kron(eye, cos)]])
    turned = plain.reshape(2, 2, n, 4 * n).transpose(1, 0, 2, 3).reshape(4 * n, 4 * n)
    rows = np.block([[cos, sin], [-sin, cos]])
    return np.stack([plain, turned]).astype(np.float32), rows.astype(np.float32)


SIGNS = np.array([[signs[1], signs[2], signs[3]] for signs in ROTATIONS], np.float32)


def split(value):
    high = value.astype(BF16)
    return high, (value - high.astype(F32)).astype(BF16)


def lane_stack(table):
    high, low = split(table)
    return jnp.concatenate([high, high, low], axis=0)


def row_stack(table):
    high, low = split(table)
    return jnp.concatenate([high, low, high], axis=1)


def lane_dot(value, table):
    high, low = split(value)
    return jnp.dot(jnp.concatenate([high, low, high], axis=1), table, preferred_element_type=F32)


def row_dot(table, value):
    high, low = split(value)
    return jnp.dot(table, jnp.concatenate([high, high, low], axis=0), preferred_element_type=F32)


def times_phase(value, cos, sin):
    re, im = value
    if im is None:
        return re * cos, -(re * sin)
    if abs(cos - sin) < 1e-12:
        return (re + im) * cos, (im - re) * cos
    return re * cos + im * sin, im * cos - re * sin


def real_forward(values):
    size = len(values)
    if size == 2:
        return [(values[0] + values[1], None), (values[0] - values[1], None)]
    even, odd = real_forward(values[0::2]), real_forward(values[1::2])
    out = [None] * (size // 2 + 1)
    out[0] = (even[0][0] + odd[0][0], None)
    out[size // 2] = (even[0][0] - odd[0][0], None)
    for k in range(1, size // 4):
        angle = 2 * math.pi * k / size
        re, im = times_phase(odd[k], math.cos(angle), math.sin(angle))
        out[k] = (even[k][0] + re, even[k][1] + im)
        out[size // 2 - k] = (even[k][0] - re, im - even[k][1])
    out[size // 4] = (even[size // 4][0], -odd[size // 4][0])
    return out


def real_inverse(spectrum):
    size = 2 * (len(spectrum) - 1)
    if size == 2:
        first, second = spectrum[0][0], spectrum[1][0]
        return [first + second, first - second]
    half, quarter = size // 2, size // 4
    even, odd = [None] * (quarter + 1), [None] * (quarter + 1)
    even[0] = (spectrum[0][0] + spectrum[half][0], None)
    odd[0] = (spectrum[0][0] - spectrum[half][0], None)
    for k in range(1, quarter):
        (ar, ai), (br, bi) = spectrum[k], spectrum[half - k]
        even[k] = (ar + br, ai - bi)
        angle = 2 * math.pi * k / size
        cos, sin = math.cos(angle), math.sin(angle)
        dr, di = ar - br, ai + bi
        if abs(cos - sin) < 1e-12:
            odd[k] = ((dr - di) * cos, (di + dr) * cos)
        else:
            odd[k] = (dr * cos - di * sin, di * cos + dr * sin)
    re, im = spectrum[quarter]
    even[quarter] = (re + re, None)
    odd[quarter] = (-(im + im), None)
    evens, odds = real_inverse(even), real_inverse(odd)
    return [value for pair in zip(evens, odds) for value in pair]


def lane_consts(width):
    left = lax.broadcasted_iota(jnp.int32, (8, width), 1) < width // 2
    one, zero = jnp.ones((8, width), F32), jnp.zeros((8, width), F32)
    return left, one, zero


def y_forward(load, count):
    width = 128
    left, one, zero = lane_consts(width)
    sign = jnp.where(left, one, -one)
    spectrum = real_forward([load(b) for b in range(count)])
    units = []
    first = spectrum[0][0]
    middle = spectrum[count // 2][0]
    units.append((first * sign + pltpu.roll(first, width // 2, 1), middle * sign))
    for k in range(1, count // 2):
        angle = 2 * math.pi * k / (2 * count)
        cos = jnp.where(left, one, math.cos(angle) * one)
        sin = jnp.where(left, zero, math.sin(angle) * one)
        re, im = spectrum[k]
        turned_re = re * cos + im * sin
        turned_im = im * cos - re * sin
        units.append(
            (
                turned_re * sign + pltpu.roll(turned_re, width // 2, 1),
                turned_im + pltpu.roll(turned_im, width // 2, 1) * sign,
            )
        )
    return units


def y_inverse(units):
    width = 128
    count = 2 * len(units)
    left, one, zero = lane_consts(width)
    sign = jnp.where(left, one, -one)
    spectrum = [None] * (count // 2 + 1)
    first, middle = units[0]
    spectrum[0] = (first * sign + pltpu.roll(first, width // 2, 1), None)
    spectrum[count // 2] = (middle * (sign + sign), None)
    for k in range(1, count // 2):
        angle = 2 * math.pi * k / (2 * count)
        cos = jnp.where(left, one, math.cos(angle) * one)
        sin = jnp.where(left, zero, math.sin(angle) * one)
        re, im = units[k]
        sum_re = re * sign + pltpu.roll(re, width // 2, 1)
        sum_im = im - pltpu.roll(im, width // 2, 1) * sign
        spectrum[k] = (sum_re * cos - sum_im * sin, sum_im * cos + sum_re * sin)
    return real_inverse(spectrum)


def forward_y_kernel(place_ref, grid_ref, mine_ref, other_ref):
    count = grid_ref.shape[1] // 128
    rows = mine_ref.shape[1]

    def run(low_ref, high_ref):
        def step(tile, carry):
            at = pl.ds(pl.multiple_of(tile * 8, 8), 8)
            units = y_forward(lambda b: grid_ref[at, b * 128 : (b + 1) * 128], count)
            half = len(units) // 2
            for k, (re, im) in enumerate(units):
                out = low_ref if k < half else high_ref
                out[2 * (k % half), at, :] = re
                out[2 * (k % half) + 1, at, :] = im
            return carry

        lax.fori_loop(0, rows // 8, step, 0, unroll=UNROLL)

    @pl.when(place_ref[0] == 0)
    def _():
        run(mine_ref, other_ref)

    @pl.when(place_ref[0] == 1)
    def _():
        run(other_ref, mine_ref)


def forward_y(place, grid):
    rows, width = grid.shape
    out = jax.ShapeDtypeStruct((width // 256, rows, 128), F32)
    return pl.pallas_call(
        forward_y_kernel,
        in_specs=[SMEM, VMEM],
        out_specs=[VMEM, VMEM],
        out_shape=[out, out],
        cost_estimate=pl.CostEstimate(flops=3 * 10**9, bytes_accessed=4 * 10**6, transcendentals=0),
        compiler_params=pltpu.CompilerParams(vmem_limit_bytes=40 * 1024 * 1024),
    )(place, grid)


RING_X, RING_Y, RING_Z = 4, 4, 8


def forward_rec_kernel(grid_ref, out_ref, rows_ref, sems):
    place = lax.axis_index("slab")
    y_hi, x = lax.axis_index("lig") // RING_X, lax.axis_index("lig") % RING_X
    share = out_ref.shape[2]
    count = grid_ref.shape[1] // 128
    copies = []
    for turn in range(COLORS):
        start = lax.rem(x + turn, COLORS) * 2 * share + y_hi * share
        rows = pl.ds(pl.multiple_of(start, share), share)
        copies.append(pltpu.make_async_copy(grid_ref.at[rows, :], rows_ref.at[turn], sems.at[turn]))
        copies[-1].start()
    def run(turn, core):
        for tile in range(share // 8):
            at = pl.ds(tile * 8, 8)
            units = y_forward(lambda b: rows_ref[turn, at, b * 128 : (b + 1) * 128], count)
            half = len(units) // 2
            for piece in range(2 * half):
                if (2 * (piece // 8) + piece) % COLORS == turn:
                    for side in range(2):
                        out_ref[piece, side ^ core, at, :] = units[half * side + piece // 2][piece % 2]

    for turn in range(COLORS):
        copies[turn].wait()
        for core in range(2):
            pl.when(place == core)(lambda turn=turn, core=core: run(turn, core))


def forward_rec(grid):
    rows, width = grid.shape
    share = rows // (2 * COLORS)
    out = jax.ShapeDtypeStruct((width // 256, 2, share, 128), F32)
    return pl.pallas_call(
        forward_rec_kernel,
        in_specs=[pl.BlockSpec(memory_space=pltpu.HBM)],
        out_specs=VMEM,
        scratch_shapes=[
            pltpu.VMEM((COLORS, share, width), F32),
            pltpu.SemaphoreType.DMA((COLORS,)),
        ],
        out_shape=out,
        compiler_params=pltpu.CompilerParams(vmem_limit_bytes=60 * 1024 * 1024),
    )(grid)


def unit_tiles(step, odd, first_re, first_im):
    left = lax.broadcasted_iota(jnp.int32, first_re.shape, 1) < first_re.shape[1] // 2
    mask = jnp.where(left, 1.0 - odd, 0.0)
    rolled = pltpu.roll(first_im, first_im.shape[1] // 2, 1)
    keep = jnp.where(step == 0, odd, 1.0)
    extra = step == STEPS - 1
    re = jnp.where(extra, first_im * mask, first_re)
    im = jnp.where(extra, rolled * mask, first_im * keep)
    return re, im


def signed(table, rows, cols, down, right, both):
    row = lax.broadcasted_iota(jnp.int32, table.shape, 0) // rows % 2 == 0
    col = lax.broadcasted_iota(jnp.int32, table.shape, 1) // cols % 2 == 0
    return table * jnp.where(row, jnp.where(col, 1.0, right), jnp.where(col, down, both))


STEPS = 9
BATCH = 9


def rows_of(lanes):
    grids = [lanes[at : at + 64] for at in range(0, lanes.shape[0], 64)]
    return jnp.concatenate(
        [jnp.concatenate([g[:, k * 128 : (k + 1) * 128] for g in grids], axis=1) for k in range(2)], axis=0
    )


def lanes_of(rows):
    return jnp.concatenate(
        [
            jnp.concatenate([rows[:64, at : at + 128], rows[64:, at : at + 128]], axis=1)
            for at in range(0, rows.shape[1], 128)
        ],
        axis=0,
    )


def spectrum_kernel(place_ref, turn_ref, signs_ref, mine_ref, other_ref, lane_ref, row_ref, out_ref, lane_work):
    place = place_ref[0]
    odd = place.astype(F32)
    channels = mine_ref.shape[1] // 32
    slots = out_ref.shape[0]
    is_low = place == 0

    def tiles(step, c):
        unit = lax.rem(step, STEPS - 1)
        at = pl.ds(c * 32, 32)
        parts = []
        for part in range(2):
            own, far = mine_ref[2 * unit + part, at, :], other_ref[2 * unit + part, at, :]
            parts.append(
                jnp.concatenate([jnp.where(is_low, own, far), jnp.where(is_low, far, own)], axis=0)
            )
        return unit_tiles(step, odd, *parts)

    for slot in range(slots):
        turn = turn_ref[slot]
        sx, sy, sz = (signs_ref[turn, k] for k in range(3))
        row_table = row_stack(signed(row_ref[...], 64, 64, sx, sx, 1.0))

        def run(swapped):
            table = signed(lane_ref[int(swapped)], 64 if swapped else 128, 128, sy * sz, sz, sy)
            lane_work[...] = lane_stack(table)

            def step(count, carry):
                grids = []
                for d in range(BATCH):
                    for c in range(channels):
                        re, im = tiles(count * BATCH + d, c)
                        if swapped:
                            turned = jnp.concatenate([re, im], axis=0).T
                            re, im = turned[:64], turned[64:]
                        grids.append(jnp.concatenate([re, im], axis=1))
                along = lane_dot(jnp.concatenate(grids, axis=0), lane_work[...])
                done = row_dot(row_table, rows_of(along))
                for d in range(BATCH):
                    for c in range(channels):
                        at = (d * channels + c) * 128
                        out_ref[slot, count * BATCH + d, c] = done[:, at : at + 128]
                return carry

            lax.fori_loop(0, STEPS // BATCH, step, 0)

        @pl.when(lax.rem(turn, 2) == 0)
        def _():
            run(False)

        @pl.when(lax.rem(turn, 2) == 1)
        def _():
            run(True)


def spectrum(place, turns, signs, mine, other, lane, row):
    pieces, rows, _ = mine.shape
    slots = turns.shape[0]
    channels = rows // 32
    return pl.pallas_call(
        spectrum_kernel,
        in_specs=[SMEM, SMEM, SMEM, VMEM, VMEM, VMEM, VMEM],
        out_specs=VMEM,
        scratch_shapes=[pltpu.VMEM((768, 256), BF16)],
        out_shape=jax.ShapeDtypeStruct((slots, STEPS, channels, 128, 128), F32),
        cost_estimate=pl.CostEstimate(flops=6 * 10**9, bytes_accessed=7 * 10**6, transcendentals=0),
        compiler_params=pltpu.CompilerParams(vmem_limit_bytes=40 * 1024 * 1024),
    )(place, turns, signs, mine, other, lane, row)


def product_kernel(
    factor, place_ref, own_ref, up_a, up_b, far_a, far_b, down_a, down_b, lig_ref, lane_ref, row_ref,
    mine_ref, other_ref, lane_work, back_work, planes,
):
    place = place_ref[0]
    odd = place.astype(F32)
    slots, steps, channels = lig_ref.shape[:3]
    lane_work[...] = lane_stack(lane_ref[0])
    back_work[...] = lane_stack(signed(lane_ref[0] * factor, 128, 128, -1.0, -1.0, 1.0))
    row_table = row_stack(row_ref[...])
    back_row = row_stack(signed(row_ref[...], 64, 64, -1.0, -1.0, 1.0))
    own = pl.ds(pl.multiple_of(place * 32, 32), 32)
    far = pl.ds(pl.multiple_of(32 - place * 32, 32), 32)
    rest = [(up_a, up_b), (far_a, far_b), (down_a, down_b)]

    def tile(turn, piece):
        if turn == 0:
            ref, at = own_ref, 2 * piece
        else:
            half = own_ref.shape[0] // 4
            ref, at = rest[turn - 1][piece // half], 2 * (piece % half)
        return jnp.concatenate([ref[at + p, s ^ place] for s in range(2) for p in range(2)], axis=0)

    grids = []
    for u in range(steps):
        unit = u % (steps - 1)
        for turn in range(channels):
            re, im = unit_tiles(u, odd, tile(turn, 2 * unit), tile(turn, 2 * unit + 1))
            grids.append(jnp.concatenate([re, im], axis=1))
    along = lane_dot(jnp.concatenate(grids, axis=0), lane_work[...])
    rec = row_dot(row_table, rows_of(along))
    sums = []
    for u in range(steps):
        for i in range(slots):
            for turn in range(channels):
                c = lax.rem(place_ref[3] + turn, channels)
                at = (u * channels + turn) * 128
                rec_re, rec_im = rec[:64, at : at + 128], rec[64:, at : at + 128]
                re, im = lig_ref[i, u, c, :64], lig_ref[i, u, c, 64:]
                term = (rec_re * re + rec_im * im, rec_re * im - rec_im * re)
                total = term if turn == 0 else (total[0] + term[0], total[1] + term[1])
            sums.append(jnp.concatenate(total, axis=0))
    rows = row_dot(back_row, jnp.concatenate(sums, axis=1))
    back = lane_dot(lanes_of(rows), back_work[...])
    parts = [back[u * slots * 64 : (u + 1) * slots * 64] for u in range(steps)]
    re, im = parts[-1][:, :128], parts[-1][:, 128:]
    left = lax.broadcasted_iota(jnp.int32, re.shape, 1) < 64
    extra = jnp.where(left, re, pltpu.roll(im, 64, 1))
    for u in range(steps - 1):
        re, im = parts[u][:, :128], parts[u][:, 128:]
        if u == 0:
            im = jnp.where(place == 0, extra, im)
        for part, value in enumerate((re, im)):
            planes[2 * u + part] = value.reshape(slots, 64, 128)
            for i in range(slots):
                mine_ref[2 * u + part, i] = planes[2 * u + part, i, own, :]
                other_ref[2 * u + part, i] = planes[2 * u + part, i, far, :]


def product(place, rec, lig, lane, row, factor):
    slots = lig.shape[0]
    pieces = 2 * (lig.shape[1] - 1)
    out = jax.ShapeDtypeStruct((pieces, slots, 32, 128), F32)
    return pl.pallas_call(
        lambda *refs: product_kernel(factor, *refs),
        in_specs=[SMEM] + [VMEM] * (len(rec) + 3),
        out_specs=[VMEM, VMEM],
        scratch_shapes=[
            pltpu.VMEM((768, 256), BF16),
            pltpu.VMEM((768, 256), BF16),
            pltpu.VMEM((pieces, slots, 64, 128), F32),
        ],
        out_shape=[out, out],
        compiler_params=pltpu.CompilerParams(vmem_limit_bytes=40 * 1024 * 1024),
    )(place, *rec, lig, lane, row)


def inverse_y_kernel(place_ref, mine_ref, other_ref, out_ref):
    pieces, slots, rows, _ = mine_ref.shape
    is_low = place_ref[0] == 0

    def step(tile, carry):
        slot = tile // (rows // 8)
        at = pl.ds(pl.multiple_of(tile % (rows // 8) * 8, 8), 8)
        low, high = [], []
        for k in range(pieces // 2):
            own = [mine_ref[2 * k + part, slot, at, :] for part in range(2)]
            far = [other_ref[2 * k + part, slot, at, :] for part in range(2)]
            low.append(tuple(jnp.where(is_low, a, b) for a, b in zip(own, far)))
            high.append(tuple(jnp.where(is_low, b, a) for a, b in zip(own, far)))
        for b, value in enumerate(y_inverse(low + high)):
            out_ref[slot, at, b * 128 : (b + 1) * 128] = value
        return carry

    lax.fori_loop(0, slots * (rows // 8), step, 0, unroll=UNROLL)


def inverse_y(place, mine, other):
    pieces, slots, rows, _ = mine.shape
    return pl.pallas_call(
        inverse_y_kernel,
        in_specs=[SMEM, VMEM, VMEM],
        out_specs=VMEM,
        out_shape=jax.ShapeDtypeStruct((slots, rows, pieces * 256), F32),
        compiler_params=pltpu.CompilerParams(vmem_limit_bytes=40 * 1024 * 1024),
    )(place, mine, other)


def color(x, y, z):
    return (x + 2 * y + z) % COLORS


def color_groups():
    return [
        [
            ((yl * RING_Z + z) * 2 * RING_X + yh * RING_X + (c - color(0, yl, z)) % RING_X) * 2 + core
            for yl in range(2)
            for z in range(RING_Z)
            for yh in range(2)
        ]
        for c in range(COLORS)
        for core in range(2)
    ]


def shift_x(step):
    return [(yh * RING_X + x, yh * RING_X + (x + step) % RING_X) for yh in range(2) for x in range(RING_X)]


def shift_y(step):
    place = lambda y, x: (y % 2) * 2 * RING_X + (y // 2) * RING_X + x
    return [(place(y, x), place((y + step) % RING_Y, x)) for y in range(RING_Y) for x in range(RING_X)]


def shift_z(step):
    return [(z, (z + step) % RING_Z) for z in range(RING_Z)]


def per_device(receptors, ligands, plan, rotations):
    _, channels, half, flat = ligands.shape
    length = 2 * half
    core = lax.axis_index("slab")
    y_hi, x = lax.axis_index("lig") // RING_X, lax.axis_index("lig") % RING_X
    tone = color(x, lax.axis_index("yl"), lax.axis_index("z"))
    place = jnp.stack([core, x, y_hi, tone]).astype(jnp.int32)
    swap = lambda value: lax.ppermute(value, "slab", [(0, 1), (1, 0)])
    lane, row = (jnp.asarray(table) for table in base_tables(length))
    signs = jnp.asarray(SIGNS)
    factor = 1.0 / (math.sqrt(channels * length**3) * length**3)

    rec_share = forward_rec(receptors.reshape(channels * half, flat))
    rec_share, root = lax.optimization_barrier((rec_share, plan[0].astype(jnp.uint32)))
    scattered = lax.all_to_all(rec_share, ("yl", "z"), split_axis=0, concat_axis=0)
    scattered, ligands = lax.optimization_barrier((scattered, ligands))
    piece = lax.dynamic_index_in_dim(scattered, root, 0, False)
    piece_far = swap(piece[1])
    lig_mine, lig_other = forward_y(place, ligands.reshape(channels * half, flat))
    piece_far, lig_mine, lig_other = lax.optimization_barrier((piece_far, lig_mine, lig_other))
    lig_far = swap(lig_other)
    piece = jnp.stack([piece[0], piece_far])[None]

    groups = color_groups()
    block = lax.all_to_all(
        jnp.broadcast_to(piece, (len(groups[0]), *piece.shape[1:])),
        ("yl", "z", "lig", "slab"),
        split_axis=0,
        concat_axis=0,
        axis_index_groups=groups,
    )
    block, lig_mine, lig_far = lax.optimization_barrier((block, lig_mine, lig_far))
    first, second = jnp.split(block, 2)
    rec = [
        block,
        lax.ppermute(first, "lig", shift_x(-1)),
        lax.ppermute(second, "z", shift_z(-1)),
        lax.ppermute(first, ("yl", "lig"), shift_y(1)),
        lax.ppermute(second, ("yl", "lig"), shift_y(-1)),
        lax.ppermute(first, "lig", shift_x(1)),
        lax.ppermute(second, "z", shift_z(1)),
    ]
    lig_spec = spectrum(place, rotations, signs, lig_mine, lig_far, lane, row)

    out_mine, out_other = product(place, rec, lig_spec, lane, row, factor)
    out_far = swap(out_other)
    scores = inverse_y(place, out_mine, out_far)
    return scores[None, :, None]


def solution(mesh):
    fine = Mesh(mesh.devices.reshape(2, RING_Z, 2 * RING_X, 2), ("yl", "z", "lig", "slab"))
    return jax.shard_map(
        per_device,
        mesh=fine,
        in_specs=(P(("yl", "z"), None, "slab", None), P(("yl", "z", "lig"), None, "slab", None), P(), P()),
        out_specs=P(None, None, ("yl", "z", "lig"), "slab", None),
        check_vma=False,
    )
```

```python
import math

import jax
import jax.numpy as jnp
import numpy as np
from jax import lax
from jax.experimental import pallas as pl
from jax.experimental.pallas import tpu as pltpu
from jax.sharding import Mesh, PartitionSpec as P

F32 = jnp.float32
BF16 = jnp.bfloat16
VMEM = pl.BlockSpec(memory_space=pltpu.VMEM)
SMEM = pl.BlockSpec(memory_space=pltpu.SMEM)
UNROLL = 4
COLORS = 4


def dft(n):
    phase = np.outer(np.arange(n), np.arange(n)) % n * (2 * math.pi / n)
    return np.cos(phase), np.sin(phase)


def base_tables(n):
    cos, sin = dft(n)
    eye = np.eye(2)
    plain = np.block([[np.kron(eye, cos), np.kron(eye, -sin)], [np.kron(eye, sin), np.kron(eye, cos)]])
    turned = plain.reshape(2, 2, n, 4 * n).transpose(1, 0, 2, 3).reshape(4 * n, 4 * n)
    rows = np.block([[cos, sin], [-sin, cos]])
    return np.stack([plain, turned]).astype(np.float32), rows.astype(np.float32)


def signs_of(turn):
    quarter, mirror = lax.rem(turn, 4), jnp.where(turn >= 4, -1.0, 1.0)
    row = jnp.where(jnp.logical_or(quarter == 1, quarter == 2), -1.0, 1.0)
    return row * mirror, mirror, jnp.where(quarter >= 2, -1.0, 1.0)


def split(value):
    high = value.astype(BF16)
    return high, (value - high.astype(F32)).astype(BF16)


def lane_stack(table):
    high, low = split(table)
    return jnp.concatenate([high, high, low], axis=0)


def row_stack(table):
    high, low = split(table)
    return jnp.concatenate([high, low, high], axis=1)


def lane_dot(value, table):
    high, low = split(value)
    return jnp.dot(jnp.concatenate([high, low, high], axis=1), table, preferred_element_type=F32)


def row_dot(table, value):
    high, low = split(value)
    return jnp.dot(table, jnp.concatenate([high, high, low], axis=0), preferred_element_type=F32)


def times_phase(value, cos, sin):
    re, im = value
    if im is None:
        return re * cos, -(re * sin)
    if abs(cos - sin) < 1e-12:
        return (re + im) * cos, (im - re) * cos
    return re * cos + im * sin, im * cos - re * sin


def real_forward(values):
    size = len(values)
    if size == 2:
        return [(values[0] + values[1], None), (values[0] - values[1], None)]
    even, odd = real_forward(values[0::2]), real_forward(values[1::2])
    out = [None] * (size // 2 + 1)
    out[0] = (even[0][0] + odd[0][0], None)
    out[size // 2] = (even[0][0] - odd[0][0], None)
    for k in range(1, size // 4):
        angle = 2 * math.pi * k / size
        re, im = times_phase(odd[k], math.cos(angle), math.sin(angle))
        out[k] = (even[k][0] + re, even[k][1] + im)
        out[size // 2 - k] = (even[k][0] - re, im - even[k][1])
    out[size // 4] = (even[size // 4][0], -odd[size // 4][0])
    return out


def real_inverse(spectrum):
    size = 2 * (len(spectrum) - 1)
    if size == 2:
        first, second = spectrum[0][0], spectrum[1][0]
        return [first + second, first - second]
    half, quarter = size // 2, size // 4
    even, odd = [None] * (quarter + 1), [None] * (quarter + 1)
    even[0] = (spectrum[0][0] + spectrum[half][0], None)
    odd[0] = (spectrum[0][0] - spectrum[half][0], None)
    for k in range(1, quarter):
        (ar, ai), (br, bi) = spectrum[k], spectrum[half - k]
        even[k] = (ar + br, ai - bi)
        angle = 2 * math.pi * k / size
        cos, sin = math.cos(angle), math.sin(angle)
        dr, di = ar - br, ai + bi
        if abs(cos - sin) < 1e-12:
            odd[k] = ((dr - di) * cos, (di + dr) * cos)
        else:
            odd[k] = (dr * cos - di * sin, di * cos + dr * sin)
    re, im = spectrum[quarter]
    even[quarter] = (re + re, None)
    odd[quarter] = (-(im + im), None)
    evens, odds = real_inverse(even), real_inverse(odd)
    return [value for pair in zip(evens, odds) for value in pair]


def lane_consts(width):
    left = lax.broadcasted_iota(jnp.int32, (8, width), 1) < width // 2
    one, zero = jnp.ones((8, width), F32), jnp.zeros((8, width), F32)
    return left, one, zero


def y_forward(load, count):
    width = 128
    left, one, zero = lane_consts(width)
    sign = jnp.where(left, one, -one)
    spectrum = real_forward([load(b) for b in range(count)])
    units = []
    first = spectrum[0][0]
    middle = spectrum[count // 2][0]
    units.append((first * sign + pltpu.roll(first, width // 2, 1), middle * sign))
    for k in range(1, count // 2):
        angle = 2 * math.pi * k / (2 * count)
        cos = jnp.where(left, one, math.cos(angle) * one)
        sin = jnp.where(left, zero, math.sin(angle) * one)
        re, im = spectrum[k]
        turned_re = re * cos + im * sin
        turned_im = im * cos - re * sin
        units.append(
            (
                turned_re * sign + pltpu.roll(turned_re, width // 2, 1),
                turned_im + pltpu.roll(turned_im, width // 2, 1) * sign,
            )
        )
    return units


def y_inverse(units):
    width = 128
    count = 2 * len(units)
    left, one, zero = lane_consts(width)
    sign = jnp.where(left, one, -one)
    spectrum = [None] * (count // 2 + 1)
    first, middle = units[0]
    spectrum[0] = (first * sign + pltpu.roll(first, width // 2, 1), None)
    spectrum[count // 2] = (middle * (sign + sign), None)
    for k in range(1, count // 2):
        angle = 2 * math.pi * k / (2 * count)
        cos = jnp.where(left, one, math.cos(angle) * one)
        sin = jnp.where(left, zero, math.sin(angle) * one)
        re, im = units[k]
        sum_re = re * sign + pltpu.roll(re, width // 2, 1)
        sum_im = im - pltpu.roll(im, width // 2, 1) * sign
        spectrum[k] = (sum_re * cos - sum_im * sin, sum_im * cos + sum_re * sin)
    return real_inverse(spectrum)


def forward_y_kernel(grid_ref, mine_ref, other_ref):
    core = lax.axis_index("slab")
    count = grid_ref.shape[1] // 128
    rows = mine_ref.shape[1]

    def run(low_ref, high_ref):
        def step(tile, carry):
            at = pl.ds(pl.multiple_of(tile * 8, 8), 8)
            units = y_forward(lambda b: grid_ref[at, b * 128 : (b + 1) * 128], count)
            half = len(units) // 2
            for k, (re, im) in enumerate(units):
                out = low_ref if k < half else high_ref
                out[2 * (k % half), at, :] = re
                out[2 * (k % half) + 1, at, :] = im
            return carry

        lax.fori_loop(0, rows // 8, step, 0, unroll=UNROLL)

    @pl.when(core == 0)
    def _():
        run(mine_ref, other_ref)

    @pl.when(core == 1)
    def _():
        run(other_ref, mine_ref)


def forward_y(grid):
    rows, width = grid.shape
    out = jax.ShapeDtypeStruct((width // 256, rows, 128), F32)
    return pl.pallas_call(
        forward_y_kernel,
        in_specs=[VMEM],
        out_specs=[VMEM, VMEM],
        out_shape=[out, out],
        cost_estimate=pl.CostEstimate(flops=3 * 10**9, bytes_accessed=4 * 10**6, transcendentals=0),
        compiler_params=pltpu.CompilerParams(vmem_limit_bytes=40 * 1024 * 1024),
    )(grid)


RING_X, RING_Y, RING_Z = 4, 4, 8


def forward_rec_kernel(grid_ref, out_ref, rows_ref, sems):
    place = lax.axis_index("slab")
    y_hi, x = lax.axis_index("lig") // RING_X, lax.axis_index("lig") % RING_X
    share = out_ref.shape[2]
    count = grid_ref.shape[1] // 128
    copies = []
    for turn in range(COLORS):
        start = lax.rem(x + turn, COLORS) * 2 * share + y_hi * share
        rows = pl.ds(pl.multiple_of(start, share), share)
        copies.append(pltpu.make_async_copy(grid_ref.at[rows, :], rows_ref.at[turn], sems.at[turn]))
        copies[-1].start()
    def run(turn, core):
        for tile in range(share // 8):
            at = pl.ds(tile * 8, 8)
            units = y_forward(lambda b: rows_ref[turn, at, b * 128 : (b + 1) * 128], count)
            half = len(units) // 2
            for piece in range(2 * half):
                if (2 * (piece // 8) + piece) % COLORS == turn:
                    for side in range(2):
                        out_ref[piece, side ^ core, at, :] = units[half * side + piece // 2][piece % 2]

    for turn in range(COLORS):
        copies[turn].wait()
        for core in range(2):
            pl.when(place == core)(lambda turn=turn, core=core: run(turn, core))


def forward_rec(grid):
    rows, width = grid.shape
    share = rows // (2 * COLORS)
    out = jax.ShapeDtypeStruct((width // 256, 2, share, 128), F32)
    return pl.pallas_call(
        forward_rec_kernel,
        in_specs=[pl.BlockSpec(memory_space=pltpu.HBM)],
        out_specs=VMEM,
        scratch_shapes=[
            pltpu.VMEM((COLORS, share, width), F32),
            pltpu.SemaphoreType.DMA((COLORS,)),
        ],
        out_shape=out,
        compiler_params=pltpu.CompilerParams(vmem_limit_bytes=60 * 1024 * 1024),
    )(grid)


def unit_tiles(step, odd, first_re, first_im):
    if step == 0:
        return first_re, first_im * odd
    if step < STEPS - 1:
        return first_re, first_im
    left = lax.broadcasted_iota(jnp.int32, first_re.shape, 1) < first_re.shape[1] // 2
    mask = jnp.where(left, 1.0 - odd, 0.0)
    return first_im * mask, pltpu.roll(first_im, first_im.shape[1] // 2, 1) * mask


def signed(table, rows, cols, down, right, both):
    row = lax.broadcasted_iota(jnp.int32, table.shape, 0) // rows % 2 == 0
    col = lax.broadcasted_iota(jnp.int32, table.shape, 1) // cols % 2 == 0
    return table * jnp.where(row, jnp.where(col, 1.0, right), jnp.where(col, down, both))


STEPS = 9
BATCH = 9
PRODUCT_BATCH = 9


def rows_of(lanes):
    grids = [lanes[at : at + 64] for at in range(0, lanes.shape[0], 64)]
    return jnp.concatenate(
        [jnp.concatenate([g[:, k * 128 : (k + 1) * 128] for g in grids], axis=1) for k in range(2)], axis=0
    )


def lanes_of(rows):
    return jnp.concatenate(
        [
            jnp.concatenate([rows[:64, at : at + 128], rows[64:, at : at + 128]], axis=1)
            for at in range(0, rows.shape[1], 128)
        ],
        axis=0,
    )


def spectrum_kernel(turn_ref, mine_ref, other_ref, lane_ref, row_ref, out_ref, lane_work):
    place = lax.axis_index("slab")
    odd = place.astype(F32)
    channels = mine_ref.shape[1] // 32
    slots = out_ref.shape[0]
    is_low = place == 0

    def tiles(step, c):
        unit = step % (STEPS - 1)
        at = pl.ds(c * 32, 32)
        parts = []
        for part in range(2):
            own, far = mine_ref[2 * unit + part, at, :], other_ref[2 * unit + part, at, :]
            parts.append(
                jnp.concatenate([jnp.where(is_low, own, far), jnp.where(is_low, far, own)], axis=0)
            )
        return unit_tiles(step, odd, *parts)

    for slot in range(slots):
        turn = turn_ref[slot]
        sx, sy, sz = signs_of(turn)
        row_table = row_stack(signed(row_ref[...], 64, 64, sx, sx, 1.0))

        def run(swapped):
            table = signed(lane_ref[int(swapped)], 64 if swapped else 128, 128, sy * sz, sz, sy)
            lane_work[...] = lane_stack(table)

            def step(count, carry):
                grids = []
                for d in range(BATCH):
                    for c in range(channels):
                        re, im = tiles(count * BATCH + d, c)
                        if swapped:
                            turned = jnp.concatenate([re, im], axis=0).T
                            re, im = turned[:64], turned[64:]
                        grids.append(jnp.concatenate([re, im], axis=1))
                along = lane_dot(jnp.concatenate(grids, axis=0), lane_work[...])
                done = row_dot(row_table, rows_of(along))
                for d in range(BATCH):
                    for c in range(channels):
                        at = (d * channels + c) * 128
                        out_ref[slot, count * BATCH + d, c] = done[:, at : at + 128]
                return carry

            for count in range(STEPS // BATCH):
                step(count, 0)

        @pl.when(lax.rem(turn, 2) == 0)
        def _():
            run(False)

        @pl.when(lax.rem(turn, 2) == 1)
        def _():
            run(True)


def spectrum(turns, mine, other, lane, row):
    pieces, rows, _ = mine.shape
    slots = turns.shape[0]
    channels = rows // 32
    return pl.pallas_call(
        spectrum_kernel,
        in_specs=[SMEM, VMEM, VMEM, VMEM, VMEM],
        out_specs=VMEM,
        scratch_shapes=[pltpu.VMEM((768, 256), BF16)],
        out_shape=jax.ShapeDtypeStruct((slots, STEPS, channels, 128, 128), F32),
        cost_estimate=pl.CostEstimate(flops=6 * 10**9, bytes_accessed=7 * 10**6, transcendentals=0),
        compiler_params=pltpu.CompilerParams(vmem_limit_bytes=40 * 1024 * 1024),
    )(turns, mine, other, lane, row)


def product_kernel(
    factor, own_ref, up_a, up_b, far_a, far_b, down_a, down_b, lig_ref, lane_ref, row_ref,
    mine_ref, other_ref, lane_work, back_work, planes,
):
    place = lax.axis_index("slab")
    odd = place.astype(F32)
    slots, steps, channels = lig_ref.shape[:3]
    tone = color(lax.axis_index("lig") % RING_X, lax.axis_index("yl"), lax.axis_index("z"))
    lane_work[...] = lane_stack(lane_ref[0])
    back_work[...] = lane_stack(signed(lane_ref[0] * factor, 128, 128, -1.0, -1.0, 1.0))
    row_table = row_stack(row_ref[...])
    back_row = row_stack(signed(row_ref[...], 64, 64, -1.0, -1.0, 1.0))
    own = pl.ds(pl.multiple_of(place * 32, 32), 32)
    far = pl.ds(pl.multiple_of(32 - place * 32, 32), 32)
    rest = [(up_a, up_b), (far_a, far_b), (down_a, down_b)]

    def tile(turn, piece):
        if turn == 0:
            ref, at = own_ref, 2 * piece
        else:
            half = own_ref.shape[0] // 4
            ref, at = rest[turn - 1][piece // half], 2 * (piece % half)
        return jnp.concatenate([ref[at + p, s ^ place] for s in range(2) for p in range(2)], axis=0)

    left = lax.broadcasted_iota(jnp.int32, (slots * 64, 128), 1) < 64
    extra = None
    order = [steps - 1, *range(steps - 1)]
    for group in (order[at : at + PRODUCT_BATCH] for at in range(0, steps, PRODUCT_BATCH)):
        grids = []
        for u in group:
            unit = u % (steps - 1)
            for turn in range(channels):
                re, im = unit_tiles(u, odd, tile(turn, 2 * unit), tile(turn, 2 * unit + 1))
                grids.append(jnp.concatenate([re, im], axis=1))
        along = lane_dot(jnp.concatenate(grids, axis=0), lane_work[...])
        rec = row_dot(row_table, rows_of(along))
        sums = []
        for d, u in enumerate(group):
            for i in range(slots):
                for turn in range(channels):
                    c = lax.rem(tone + turn, channels)
                    at = (d * channels + turn) * 128
                    rec_re, rec_im = rec[:64, at : at + 128], rec[64:, at : at + 128]
                    re, im = lig_ref[i, u, c, :64], lig_ref[i, u, c, 64:]
                    term = (rec_re * re + rec_im * im, rec_re * im - rec_im * re)
                    total = term if turn == 0 else (total[0] + term[0], total[1] + term[1])
                sums.append(jnp.concatenate(total, axis=0))
        rows = row_dot(back_row, jnp.concatenate(sums, axis=1))
        back = lane_dot(lanes_of(rows), back_work[...])
        for d, u in enumerate(group):
            part = back[d * slots * 64 : (d + 1) * slots * 64]
            re, im = part[:, :128], part[:, 128:]
            if u == steps - 1:
                extra = jnp.where(left, re, pltpu.roll(im, 64, 1))
                continue
            if u == 0:
                im = jnp.where(place == 0, extra, im)
            for half, value in enumerate((re, im)):
                planes[2 * u + half] = value.reshape(slots, 64, 128)
                for i in range(slots):
                    mine_ref[2 * u + half, i] = planes[2 * u + half, i, own, :]
                    other_ref[2 * u + half, i] = planes[2 * u + half, i, far, :]


def product(rec, lig, lane, row, factor):
    slots = lig.shape[0]
    pieces = 2 * (lig.shape[1] - 1)
    out = jax.ShapeDtypeStruct((pieces, slots, 32, 128), F32)
    return pl.pallas_call(
        lambda *refs: product_kernel(factor, *refs),
        in_specs=[VMEM] * (len(rec) + 3),
        out_specs=[VMEM, VMEM],
        scratch_shapes=[
            pltpu.VMEM((768, 256), BF16),
            pltpu.VMEM((768, 256), BF16),
            pltpu.VMEM((pieces, slots, 64, 128), F32),
        ],
        out_shape=[out, out],
        compiler_params=pltpu.CompilerParams(vmem_limit_bytes=40 * 1024 * 1024),
    )(*rec, lig, lane, row)


def inverse_y_kernel(mine_ref, other_ref, out_ref):
    pieces, _, rows, _ = mine_ref.shape
    is_low = lax.axis_index("slab") == 0
    slot = pl.program_id(0)

    def step(tile, carry):
        at = pl.ds(pl.multiple_of(tile * 8, 8), 8)
        low, high = [], []
        for k in range(pieces // 2):
            own = [mine_ref[2 * k + part, slot, at, :] for part in range(2)]
            far = [other_ref[2 * k + part, slot, at, :] for part in range(2)]
            low.append(tuple(jnp.where(is_low, a, b) for a, b in zip(own, far)))
            high.append(tuple(jnp.where(is_low, b, a) for a, b in zip(own, far)))
        for b, value in enumerate(y_inverse(low + high)):
            out_ref[0, at, b * 128 : (b + 1) * 128] = value
        return carry

    lax.fori_loop(0, rows // 8, step, 0, unroll=UNROLL)


def inverse_y(mine, other):
    pieces, slots, rows, _ = mine.shape
    return pl.pallas_call(
        inverse_y_kernel,
        grid=(slots,),
        in_specs=[VMEM, VMEM],
        out_specs=pl.BlockSpec((1, rows, pieces * 256), lambda i: (i, 0, 0)),
        out_shape=jax.ShapeDtypeStruct((slots, rows, pieces * 256), F32),
        compiler_params=pltpu.CompilerParams(vmem_limit_bytes=40 * 1024 * 1024),
    )(mine, other)


def color(x, y, z):
    return (x + 2 * y + z) % COLORS


def color_groups():
    return [
        [
            ((yl * RING_Z + z) * 2 * RING_X + yh * RING_X + (c - color(0, yl, z)) % RING_X) * 2 + core
            for yl in range(2)
            for z in range(RING_Z)
            for yh in range(2)
        ]
        for c in range(COLORS)
        for core in range(2)
    ]


def shift_x(step):
    return [(yh * RING_X + x, yh * RING_X + (x + step) % RING_X) for yh in range(2) for x in range(RING_X)]


def shift_y(step):
    place = lambda y, x: (y % 2) * 2 * RING_X + (y // 2) * RING_X + x
    return [(place(y, x), place((y + step) % RING_Y, x)) for y in range(RING_Y) for x in range(RING_X)]


def shift_z(step):
    return [(z, (z + step) % RING_Z) for z in range(RING_Z)]


def per_device(receptors, ligands, plan, rotations):
    _, channels, half, flat = ligands.shape
    length = 2 * half
    swap = lambda value: lax.ppermute(value, "slab", [(0, 1), (1, 0)])
    lane, row = (jnp.asarray(table) for table in base_tables(length))
    factor = 1.0 / (math.sqrt(channels * length**3) * length**3)

    rec_share = forward_rec(receptors.reshape(channels * half, flat))
    scattered = lax.all_to_all(rec_share, ("yl", "z"), split_axis=0, concat_axis=0)
    scattered, ligands = lax.optimization_barrier((scattered, ligands))
    piece = lax.dynamic_index_in_dim(scattered, plan[0], 0, False)
    piece_far = swap(piece[1])
    lig_mine, lig_other = forward_y(ligands.reshape(channels * half, flat))
    piece_far, lig_mine, lig_other = lax.optimization_barrier((piece_far, lig_mine, lig_other))
    lig_far = swap(lig_other)
    piece = jnp.stack([piece[0], piece_far])[None]

    groups = color_groups()
    block = lax.all_to_all(
        jnp.broadcast_to(piece, (len(groups[0]), *piece.shape[1:])),
        ("yl", "z", "lig", "slab"),
        split_axis=0,
        concat_axis=0,
        axis_index_groups=groups,
    )
    block, lig_mine, lig_far = lax.optimization_barrier((block, lig_mine, lig_far))
    first, second = jnp.split(block, 2)
    rec = [
        block,
        lax.ppermute(first, "lig", shift_x(-1)),
        lax.ppermute(second, "z", shift_z(-1)),
        lax.ppermute(first, ("yl", "lig"), shift_y(1)),
        lax.ppermute(second, ("yl", "lig"), shift_y(-1)),
        lax.ppermute(first, "lig", shift_x(1)),
        lax.ppermute(second, "z", shift_z(1)),
    ]
    lig_spec = spectrum(rotations, lig_mine, lig_far, lane, row)

    out_mine, out_other = product(rec, lig_spec, lane, row, factor)
    out_far = swap(out_other)
    scores = inverse_y(out_mine, out_far)
    return scores[None, :, None]


def solution(mesh):
    fine = Mesh(mesh.devices.reshape(2, RING_Z, 2 * RING_X, 2), ("yl", "z", "lig", "slab"))
    return jax.shard_map(
        per_device,
        mesh=fine,
        in_specs=(P(("yl", "z"), None, "slab", None), P(("yl", "z", "lig"), None, "slab", None), P(), P()),
        out_specs=P(None, None, ("yl", "z", "lig"), "slab", None),
        check_vma=False,
    )
```

```python
import math

import jax
import jax.numpy as jnp
import numpy as np
from jax import lax
from jax.experimental import pallas as pl
from jax.experimental.pallas import tpu as pltpu
from jax.sharding import Mesh, PartitionSpec as P

F32 = jnp.float32
BF16 = jnp.bfloat16
VMEM = pl.BlockSpec(memory_space=pltpu.VMEM)
SMEM = pl.BlockSpec(memory_space=pltpu.SMEM)
UNROLL = 4
COLORS = 4


def dft(n):
    phase = np.outer(np.arange(n), np.arange(n)) % n * (2 * math.pi / n)
    return np.cos(phase), np.sin(phase)


def base_tables(n):
    cos, sin = dft(n)
    eye = np.eye(2)
    plain = np.block([[np.kron(eye, cos), np.kron(eye, -sin)], [np.kron(eye, sin), np.kron(eye, cos)]])
    turned = plain.reshape(2, 2, n, 4 * n).transpose(1, 0, 2, 3).reshape(4 * n, 4 * n)
    rows = np.block([[cos, sin], [-sin, cos]])
    return np.stack([plain, turned]).astype(np.float32), rows.astype(np.float32)


def signs_of(turn):
    quarter, mirror = lax.rem(turn, 4), jnp.where(turn >= 4, -1.0, 1.0)
    row = jnp.where(jnp.logical_or(quarter == 1, quarter == 2), -1.0, 1.0)
    return row * mirror, mirror, jnp.where(quarter >= 2, -1.0, 1.0)


def split(value):
    high = value.astype(BF16)
    return high, (value - high.astype(F32)).astype(BF16)


def lane_stack(table):
    high, low = split(table)
    return jnp.concatenate([high, high, low], axis=0)


def row_stack(table):
    high, low = split(table)
    return jnp.concatenate([high, low, high], axis=1)


def lane_dot(value, table):
    high, low = split(value)
    return jnp.dot(jnp.concatenate([high, low, high], axis=1), table, preferred_element_type=F32)


def row_dot(table, value):
    high, low = split(value)
    return jnp.dot(table, jnp.concatenate([high, high, low], axis=0), preferred_element_type=F32)


def times_phase(value, cos, sin):
    re, im = value
    if im is None:
        return re * cos, -(re * sin)
    if abs(cos - sin) < 1e-12:
        return (re + im) * cos, (im - re) * cos
    return re * cos + im * sin, im * cos - re * sin


def real_forward(values):
    size = len(values)
    if size == 2:
        return [(values[0] + values[1], None), (values[0] - values[1], None)]
    even, odd = real_forward(values[0::2]), real_forward(values[1::2])
    out = [None] * (size // 2 + 1)
    out[0] = (even[0][0] + odd[0][0], None)
    out[size // 2] = (even[0][0] - odd[0][0], None)
    for k in range(1, size // 4):
        angle = 2 * math.pi * k / size
        re, im = times_phase(odd[k], math.cos(angle), math.sin(angle))
        out[k] = (even[k][0] + re, even[k][1] + im)
        out[size // 2 - k] = (even[k][0] - re, im - even[k][1])
    out[size // 4] = (even[size // 4][0], -odd[size // 4][0])
    return out


def real_inverse(spectrum):
    size = 2 * (len(spectrum) - 1)
    if size == 2:
        first, second = spectrum[0][0], spectrum[1][0]
        return [first + second, first - second]
    half, quarter = size // 2, size // 4
    even, odd = [None] * (quarter + 1), [None] * (quarter + 1)
    even[0] = (spectrum[0][0] + spectrum[half][0], None)
    odd[0] = (spectrum[0][0] - spectrum[half][0], None)
    for k in range(1, quarter):
        (ar, ai), (br, bi) = spectrum[k], spectrum[half - k]
        even[k] = (ar + br, ai - bi)
        angle = 2 * math.pi * k / size
        cos, sin = math.cos(angle), math.sin(angle)
        dr, di = ar - br, ai + bi
        if abs(cos - sin) < 1e-12:
            odd[k] = ((dr - di) * cos, (di + dr) * cos)
        else:
            odd[k] = (dr * cos - di * sin, di * cos + dr * sin)
    re, im = spectrum[quarter]
    even[quarter] = (re + re, None)
    odd[quarter] = (-(im + im), None)
    evens, odds = real_inverse(even), real_inverse(odd)
    return [value for pair in zip(evens, odds) for value in pair]


def lane_consts(width):
    left = lax.broadcasted_iota(jnp.int32, (8, width), 1) < width // 2
    one, zero = jnp.ones((8, width), F32), jnp.zeros((8, width), F32)
    return left, one, zero


def y_forward(load, count):
    width = 128
    left, one, zero = lane_consts(width)
    sign = jnp.where(left, one, -one)
    spectrum = real_forward([load(b) for b in range(count)])
    units = []
    first = spectrum[0][0]
    middle = spectrum[count // 2][0]
    units.append((first * sign + pltpu.roll(first, width // 2, 1), middle * sign))
    for k in range(1, count // 2):
        angle = 2 * math.pi * k / (2 * count)
        cos = jnp.where(left, one, math.cos(angle) * one)
        sin = jnp.where(left, zero, math.sin(angle) * one)
        re, im = spectrum[k]
        turned_re = re * cos + im * sin
        turned_im = im * cos - re * sin
        units.append(
            (
                turned_re * sign + pltpu.roll(turned_re, width // 2, 1),
                turned_im + pltpu.roll(turned_im, width // 2, 1) * sign,
            )
        )
    return units


def y_inverse(units):
    width = 128
    count = 2 * len(units)
    left, one, zero = lane_consts(width)
    sign = jnp.where(left, one, -one)
    spectrum = [None] * (count // 2 + 1)
    first, middle = units[0]
    spectrum[0] = (first * sign + pltpu.roll(first, width // 2, 1), None)
    spectrum[count // 2] = (middle * (sign + sign), None)
    for k in range(1, count // 2):
        angle = 2 * math.pi * k / (2 * count)
        cos = jnp.where(left, one, math.cos(angle) * one)
        sin = jnp.where(left, zero, math.sin(angle) * one)
        re, im = units[k]
        sum_re = re * sign + pltpu.roll(re, width // 2, 1)
        sum_im = im - pltpu.roll(im, width // 2, 1) * sign
        spectrum[k] = (sum_re * cos - sum_im * sin, sum_im * cos + sum_re * sin)
    return real_inverse(spectrum)


def forward_y_kernel(grid_ref, mine_ref, other_ref):
    core = lax.axis_index("slab")
    count = grid_ref.shape[1] // 128
    rows = mine_ref.shape[1]

    def run(low_ref, high_ref):
        def step(tile, carry):
            at = pl.ds(pl.multiple_of(tile * 8, 8), 8)
            units = y_forward(lambda b: grid_ref[at, b * 128 : (b + 1) * 128], count)
            half = len(units) // 2
            for k, (re, im) in enumerate(units):
                out = low_ref if k < half else high_ref
                out[2 * (k % half), at, :] = re
                out[2 * (k % half) + 1, at, :] = im
            return carry

        lax.fori_loop(0, rows // 8, step, 0, unroll=UNROLL)

    @pl.when(core == 0)
    def _():
        run(mine_ref, other_ref)

    @pl.when(core == 1)
    def _():
        run(other_ref, mine_ref)


def forward_y(grid):
    rows, width = grid.shape
    out = jax.ShapeDtypeStruct((width // 256, rows, 128), F32)
    return pl.pallas_call(
        forward_y_kernel,
        in_specs=[VMEM],
        out_specs=[VMEM, VMEM],
        out_shape=[out, out],
        cost_estimate=pl.CostEstimate(flops=3 * 10**9, bytes_accessed=4 * 10**6, transcendentals=0),
        compiler_params=pltpu.CompilerParams(vmem_limit_bytes=40 * 1024 * 1024),
    )(grid)


RING_X, RING_Z = 4, 8


def forward_rec_kernel(grid_ref, out_ref, rows_ref, sems):
    place = lax.axis_index("slab")
    y_hi, x = lax.axis_index("lig") // RING_X, lax.axis_index("lig") % RING_X
    share = out_ref.shape[2]
    count = grid_ref.shape[1] // 128
    copies = []
    for turn in range(COLORS):
        start = lax.rem(x + turn, COLORS) * 2 * share + y_hi * share
        rows = pl.ds(pl.multiple_of(start, share), share)
        copies.append(pltpu.make_async_copy(grid_ref.at[rows, :], rows_ref.at[turn], sems.at[turn]))
        copies[-1].start()
    def run(turn, core):
        for tile in range(share // 8):
            at = pl.ds(tile * 8, 8)
            units = y_forward(lambda b: rows_ref[turn, at, b * 128 : (b + 1) * 128], count)
            half = len(units) // 2
            for piece in range(2 * half):
                if (2 * (piece // 8) + piece) % COLORS == turn:
                    for side in range(2):
                        out_ref[piece, side ^ core, at, :] = units[half * side + piece // 2][piece % 2]

    for turn in range(COLORS):
        copies[turn].wait()
        for core in range(2):
            pl.when(place == core)(lambda turn=turn, core=core: run(turn, core))


def forward_rec(grid):
    rows, width = grid.shape
    share = rows // (2 * COLORS)
    out = jax.ShapeDtypeStruct((width // 256, 2, share, 128), F32)
    return pl.pallas_call(
        forward_rec_kernel,
        in_specs=[pl.BlockSpec(memory_space=pltpu.HBM)],
        out_specs=VMEM,
        scratch_shapes=[
            pltpu.VMEM((COLORS, share, width), F32),
            pltpu.SemaphoreType.DMA((COLORS,)),
        ],
        out_shape=out,
        compiler_params=pltpu.CompilerParams(vmem_limit_bytes=60 * 1024 * 1024),
    )(grid)


def unit_tiles(step, odd, first_re, first_im):
    if step == 0:
        return first_re, first_im * odd
    if step < STEPS - 1:
        return first_re, first_im
    left = lax.broadcasted_iota(jnp.int32, first_re.shape, 1) < first_re.shape[1] // 2
    mask = jnp.where(left, 1.0 - odd, 0.0)
    return first_im * mask, pltpu.roll(first_im, first_im.shape[1] // 2, 1) * mask


def signed(table, rows, cols, down, right, both):
    row = lax.broadcasted_iota(jnp.int32, table.shape, 0) // rows % 2 == 0
    col = lax.broadcasted_iota(jnp.int32, table.shape, 1) // cols % 2 == 0
    return table * jnp.where(row, jnp.where(col, 1.0, right), jnp.where(col, down, both))


STEPS = 9
BATCH = 9
PRODUCT_BATCH = 9


def rows_of(lanes):
    grids = [lanes[at : at + 64] for at in range(0, lanes.shape[0], 64)]
    return jnp.concatenate(
        [jnp.concatenate([g[:, k * 128 : (k + 1) * 128] for g in grids], axis=1) for k in range(2)], axis=0
    )


def lanes_of(rows):
    return jnp.concatenate(
        [
            jnp.concatenate([rows[:64, at : at + 128], rows[64:, at : at + 128]], axis=1)
            for at in range(0, rows.shape[1], 128)
        ],
        axis=0,
    )


def spectrum_kernel(turn_ref, mine_ref, other_ref, lane_ref, row_ref, out_ref, lane_work):
    place = lax.axis_index("slab")
    odd = place.astype(F32)
    channels = mine_ref.shape[1] // 32
    slots = out_ref.shape[0]
    is_low = place == 0

    def tiles(step, c):
        unit = step % (STEPS - 1)
        at = pl.ds(c * 32, 32)
        parts = []
        for part in range(2):
            own, far = mine_ref[2 * unit + part, at, :], other_ref[2 * unit + part, at, :]
            parts.append(
                jnp.concatenate([jnp.where(is_low, own, far), jnp.where(is_low, far, own)], axis=0)
            )
        return unit_tiles(step, odd, *parts)

    for slot in range(slots):
        turn = turn_ref[slot]
        sx, sy, sz = signs_of(turn)
        row_table = row_stack(signed(row_ref[...], 64, 64, sx, sx, 1.0))

        def run(swapped):
            table = signed(lane_ref[int(swapped)], 64 if swapped else 128, 128, sy * sz, sz, sy)
            lane_work[...] = lane_stack(table)

            def step(count, carry):
                grids = []
                for d in range(BATCH):
                    for c in range(channels):
                        re, im = tiles(count * BATCH + d, c)
                        if swapped:
                            turned = jnp.concatenate([re, im], axis=0).T
                            re, im = turned[:64], turned[64:]
                        grids.append(jnp.concatenate([re, im], axis=1))
                along = lane_dot(jnp.concatenate(grids, axis=0), lane_work[...])
                done = row_dot(row_table, rows_of(along))
                for d in range(BATCH):
                    for c in range(channels):
                        at = (d * channels + c) * 128
                        out_ref[slot, count * BATCH + d, c] = done[:, at : at + 128]
                return carry

            for count in range(STEPS // BATCH):
                step(count, 0)

        @pl.when(lax.rem(turn, 2) == 0)
        def _():
            run(False)

        @pl.when(lax.rem(turn, 2) == 1)
        def _():
            run(True)


def spectrum(turns, mine, other, lane, row):
    pieces, rows, _ = mine.shape
    slots = turns.shape[0]
    channels = rows // 32
    return pl.pallas_call(
        spectrum_kernel,
        in_specs=[SMEM, VMEM, VMEM, VMEM, VMEM],
        out_specs=VMEM,
        scratch_shapes=[pltpu.VMEM((768, 256), BF16)],
        out_shape=jax.ShapeDtypeStruct((slots, STEPS, channels, 128, 128), F32),
        compiler_params=pltpu.CompilerParams(vmem_limit_bytes=40 * 1024 * 1024),
    )(turns, mine, other, lane, row)


def product_kernel(
    factor, own_ref, up_a, up_b, far_ref, down_a, down_b, lig_ref, lane_ref, row_ref,
    mine_ref, other_ref, lane_work, back_work, planes,
):
    place = lax.axis_index("slab")
    odd = place.astype(F32)
    slots, steps, channels = lig_ref.shape[:3]
    tone = color(lax.axis_index("lig") % RING_X, lax.axis_index("yl"), lax.axis_index("z"))
    lane_work[...] = lane_stack(lane_ref[0])
    back_work[...] = lane_stack(signed(lane_ref[0] * factor, 128, 128, -1.0, -1.0, 1.0))
    row_table = row_stack(row_ref[...])
    back_row = row_stack(signed(row_ref[...], 64, 64, -1.0, -1.0, 1.0))
    own = pl.ds(pl.multiple_of(place * 32, 32), 32)
    far = pl.ds(pl.multiple_of(32 - place * 32, 32), 32)
    held = [own_ref, (up_a, up_b), far_ref, (down_a, down_b)]

    def tile(turn, piece):
        ref, at = held[turn], 2 * piece
        if isinstance(ref, tuple):
            half = ref[0].shape[0]
            ref, at = ref[at // half], at % half
        return jnp.concatenate([ref[at + p, s ^ place] for s in range(2) for p in range(2)], axis=0)

    left = lax.broadcasted_iota(jnp.int32, (slots * 64, 128), 1) < 64
    extra = None
    order = [steps - 1, *range(steps - 1)]
    for group in (order[at : at + PRODUCT_BATCH] for at in range(0, steps, PRODUCT_BATCH)):
        grids = []
        for u in group:
            unit = u % (steps - 1)
            for turn in range(channels):
                re, im = unit_tiles(u, odd, tile(turn, 2 * unit), tile(turn, 2 * unit + 1))
                grids.append(jnp.concatenate([re, im], axis=1))
        along = lane_dot(jnp.concatenate(grids, axis=0), lane_work[...])
        rec = row_dot(row_table, rows_of(along))
        sums = []
        for d, u in enumerate(group):
            for i in range(slots):
                for turn in range(channels):
                    c = lax.rem(tone + turn, channels)
                    at = (d * channels + turn) * 128
                    rec_re, rec_im = rec[:64, at : at + 128], rec[64:, at : at + 128]
                    re, im = lig_ref[i, u, c, :64], lig_ref[i, u, c, 64:]
                    term = (rec_re * re + rec_im * im, rec_re * im - rec_im * re)
                    total = term if turn == 0 else (total[0] + term[0], total[1] + term[1])
                sums.append(jnp.concatenate(total, axis=0))
        rows = row_dot(back_row, jnp.concatenate(sums, axis=1))
        back = lane_dot(lanes_of(rows), back_work[...])
        for d, u in enumerate(group):
            part = back[d * slots * 64 : (d + 1) * slots * 64]
            re, im = part[:, :128], part[:, 128:]
            if u == steps - 1:
                extra = jnp.where(left, re, pltpu.roll(im, 64, 1))
                continue
            if u == 0:
                im = jnp.where(place == 0, extra, im)
            for half, value in enumerate((re, im)):
                planes[2 * u + half] = value.reshape(slots, 64, 128)
                for i in range(slots):
                    mine_ref[2 * u + half, i] = planes[2 * u + half, i, own, :]
                    other_ref[2 * u + half, i] = planes[2 * u + half, i, far, :]


def product(rec, lig, lane, row, factor):
    slots = lig.shape[0]
    pieces = 2 * (lig.shape[1] - 1)
    out = jax.ShapeDtypeStruct((pieces, slots, 32, 128), F32)
    return pl.pallas_call(
        lambda *refs: product_kernel(factor, *refs),
        in_specs=[VMEM] * (len(rec) + 3),
        out_specs=[VMEM, VMEM],
        scratch_shapes=[
            pltpu.VMEM((768, 256), BF16),
            pltpu.VMEM((768, 256), BF16),
            pltpu.VMEM((pieces, slots, 64, 128), F32),
        ],
        out_shape=[out, out],
        compiler_params=pltpu.CompilerParams(vmem_limit_bytes=40 * 1024 * 1024),
    )(*rec, lig, lane, row)


def inverse_y_kernel(mine_ref, other_ref, out_ref):
    pieces, _, rows, _ = mine_ref.shape
    is_low = lax.axis_index("slab") == 0
    slot = pl.program_id(0)

    def step(tile, carry):
        at = pl.ds(pl.multiple_of(tile * 8, 8), 8)
        low, high = [], []
        for k in range(pieces // 2):
            own = [mine_ref[2 * k + part, slot, at, :] for part in range(2)]
            far = [other_ref[2 * k + part, slot, at, :] for part in range(2)]
            low.append(tuple(jnp.where(is_low, a, b) for a, b in zip(own, far)))
            high.append(tuple(jnp.where(is_low, b, a) for a, b in zip(own, far)))
        for b, value in enumerate(y_inverse(low + high)):
            out_ref[0, at, b * 128 : (b + 1) * 128] = value
        return carry

    lax.fori_loop(0, rows // 8, step, 0, unroll=UNROLL)


def inverse_y(mine, other):
    pieces, slots, rows, _ = mine.shape
    return pl.pallas_call(
        inverse_y_kernel,
        grid=(slots,),
        in_specs=[VMEM, VMEM],
        out_specs=pl.BlockSpec((1, rows, pieces * 256), lambda i: (i, 0, 0)),
        out_shape=jax.ShapeDtypeStruct((slots, rows, pieces * 256), F32),
        compiler_params=pltpu.CompilerParams(vmem_limit_bytes=40 * 1024 * 1024),
    )(mine, other)


def color(x, y, z):
    return (x + 2 * y + z) % COLORS


def color_groups():
    return [
        [
            ((yl * RING_Z + z) * 2 * RING_X + yh * RING_X + (c - color(0, yl, z)) % RING_X) * 2 + core
            for yl in range(2)
            for z in range(RING_Z)
            for yh in range(2)
        ]
        for c in range(COLORS)
        for core in range(2)
    ]


def shift_x(step):
    return [(yh * RING_X + x, yh * RING_X + (x + step) % RING_X) for yh in range(2) for x in range(RING_X)]


def shift_z(step):
    return [(z, (z + step) % RING_Z) for z in range(RING_Z)]


def per_device(receptors, ligands, plan, rotations):
    _, channels, half, flat = ligands.shape
    length = 2 * half
    swap = lambda value: lax.ppermute(value, "slab", [(0, 1), (1, 0)])
    lane, row = (jnp.asarray(table) for table in base_tables(length))
    factor = 1.0 / (math.sqrt(channels * length**3) * length**3)

    rec_share = forward_rec(receptors.reshape(channels * half, flat))
    scattered = lax.all_to_all(rec_share, ("yl", "z"), split_axis=0, concat_axis=0)
    scattered, ligands = lax.optimization_barrier((scattered, ligands))
    piece = lax.dynamic_index_in_dim(scattered, plan[0], 0, False)
    piece_far = swap(piece[1])
    lig_mine, lig_other = forward_y(ligands.reshape(channels * half, flat))
    piece_far, lig_mine, lig_other = lax.optimization_barrier((piece_far, lig_mine, lig_other))
    lig_far = swap(lig_other)
    piece = jnp.stack([piece[0], piece_far])[None]

    groups = color_groups()
    block = lax.all_to_all(
        jnp.broadcast_to(piece, (len(groups[0]), *piece.shape[1:])),
        ("yl", "z", "lig", "slab"),
        split_axis=0,
        concat_axis=0,
        axis_index_groups=groups,
    )
    block, lig_mine, lig_far = lax.optimization_barrier((block, lig_mine, lig_far))
    first, second = jnp.split(block, 2)
    rec = [
        block,
        lax.ppermute(first, "lig", shift_x(-1)),
        lax.ppermute(second, "z", shift_z(-1)),
        lax.ppermute(block, "yl", [(0, 1), (1, 0)]),
        lax.ppermute(first, "lig", shift_x(1)),
        lax.ppermute(second, "z", shift_z(1)),
    ]
    lig_spec = spectrum(rotations, lig_mine, lig_far, lane, row)

    out_mine, out_other = product(rec, lig_spec, lane, row, factor)
    out_far = swap(out_other)
    scores = inverse_y(out_mine, out_far)
    return scores[None, :, None]


def solution(mesh):
    fine = Mesh(mesh.devices.reshape(2, RING_Z, 2 * RING_X, 2), ("yl", "z", "lig", "slab"))
    return jax.shard_map(
        per_device,
        mesh=fine,
        in_specs=(P(("yl", "z"), None, "slab", None), P(("yl", "z", "lig"), None, "slab", None), P(), P()),
        out_specs=P(None, None, ("yl", "z", "lig"), "slab", None),
        check_vma=False,
    )
```
